128 devices in a mesh: dp: 16 (over y_lo, z, core), seq: 8 (over x, y_hi).
Axes of the slice: x: 4, y: 4 (y_hi: 2, y_lo: 2; y = y_hi * 2 + y_lo), z: 4, core: 2. Of those that a mesh axis runs over, the one named last changes fastest.
Arguments:
- inputs: bfloat16 [16, 8, 8, 16, 1536], P('dp', 'seq'), may hold values from -6 to 6
- spatial_q: bfloat16 [16, 8, 8, 16, 1536], P('dp', 'seq'), may hold values from -68 to 68
- spatial_k: bfloat16 [16, 8, 8, 16, 1536], P('dp', 'seq'), may hold values from -4 to 4
- spatial_v: bfloat16 [16, 8, 8, 16, 1536], P('dp', 'seq'), may hold values from -6 to 6
- out_weight: bfloat16 [1536, 1536], P('dp'), may hold values from -0.15625 to 0.15625
- norm_gain: float32 [1536], replicated, may hold values from 0.1 to 1.9
- qkv_weight: bfloat16 [1536, 4608], P('dp', 'seq')
- grad_out: bfloat16 [16, 8, 8, 16, 1536], P('dp', 'seq'), may hold values from -6 to 6
- grad_resid: bfloat16 [16, 8, 8, 16, 1536], P('dp', 'seq'), may hold values from -6 to 6
Outputs:
- hidden: bfloat16 [16, 8, 8, 16, 1536], P('dp', 'seq')
- temporal_out: bfloat16 [16, 8, 8, 16, 1536], P('dp', 'seq')
- grad_input: bfloat16 [16, 8, 8, 16, 1536], P('dp', 'seq')
- grad_spatial_q: bfloat16 [16, 8, 8, 16, 1536], P('dp', 'seq')
- grad_spatial_k: bfloat16 [16, 8, 8, 16, 1536], P('dp', 'seq')
- grad_spatial_v: bfloat16 [16, 8, 8, 16, 1536], P('dp', 'seq')
- qkv_grad: float32 [1536, 4608], P('dp', 'seq')
- out_grad: float32 [1536, 1536], P('dp')
- gain_grad: float32 [1536], replicated
The draws below stay inside these ranges and needn't reach their ends.
All inputs are finite; a program needn't handle non-finite values.
Results may differ from the reference program's by a relative error of at most 0.03.
Values may be sent and summed in bfloat16 or wider, within the bound.
No kernel may reach another device: no remote copies, remote signals or barrier semaphores. Data moves between devices by JAX's collectives and lax.ppermute only.
A program may use at most 128 MiB of HBM per device.

```python
import jax
import jax.numpy as jnp
from jax import lax

D = 1536
HEADS = 24
HDIM = 64
ROWS = 8
COLS = 16
FRAMES = 8
CLIPS = 16
E = 1536
N_DP = 16


def normal_frames(key, code):
    array_shape = (N_DP, FRAMES, ROWS * COLS, HEADS, HDIM)
    return jnp.clip(jax.random.normal(jax.random.fold_in(key, code), array_shape, jnp.float32), -4.0, 4.0)


def draw_spatial_k(key, part):
    drawn = normal_frames(key, 21)
    return drawn.reshape(N_DP, FRAMES, ROWS, COLS, HEADS * HDIM).astype(jnp.bfloat16)


def draw_spatial_q(key, part):
    key = jax.random.fold_in(key, 3)
    own_draw = normal_frames(key, 5)
    return own_draw.reshape(N_DP, FRAMES, ROWS, COLS, HEADS * HDIM).astype(jnp.bfloat16)


def draw_qkv_weight(key, part):
    key = jax.random.fold_in(key, 9)
    array_shape = (D, HEADS, 3, HDIM)
    drawn = jnp.clip(jax.random.normal(key, array_shape, jnp.float32), -4.0, 4.0) * D ** (-0.5)
    return drawn.reshape(D, 3 * HEADS * HDIM).astype(jnp.bfloat16)


def with_spikes(values, own_key, source, target, shards_of, factor):
    owner, partner = [(jnp.arange(values.shape[axis_at]) // (values.shape[axis_at] // shards_of)).reshape([-1 if axis == axis_at else 1 for axis in range(values.ndim)]) for axis_at in (source, target)]
    chosen = jax.random.permutation(own_key, shards_of)[partner]
    strong = (owner == chosen) | (owner == (partner + shards_of // 2) % shards_of)
    return jnp.where(strong, factor * values, values)


def levels(rng, extent, shards, smallest, largest):
    def one(axis_at, blocks):
        heights = jax.random.uniform(jax.random.fold_in(jax.random.fold_in(rng, 6), axis_at), (blocks,), jnp.float32, smallest / len(shards), largest / len(shards))
        return jnp.repeat(jnp.exp(heights), extent[axis_at] // blocks).reshape((-1,) + (1,) * (len(extent) - axis_at - 1))

    gain = one(*shards[0])
    for cut in shards[1:]:
        gain = gain * one(*cut)
    return gain


def bell_draw(own_key, extent, scale, limit, split=(), dtype=jnp.bfloat16):
    gain = levels(own_key, extent, split, -0.22, 0.18) if split else 1.0
    values = jax.random.normal(own_key, extent, jnp.float32) * scale * gain
    return jnp.minimum(jnp.maximum(values, -limit), limit).astype(dtype)


def gaussian_with(key, dims, scale, limit, split, heavy, kind=jnp.bfloat16):
    entries = scale * jax.random.normal(key, dims, jnp.float32)
    if split:
        entries = entries * levels(key, dims, split, -0.22, 0.18)
    return jnp.clip(with_spikes(entries, jax.random.fold_in(key, 3), *heavy), -limit, limit).astype(kind)


def setup_inputs(seed: int = 0) -> dict:
    arg_keys = jax.random.split(jax.random.key(seed), 10)
    inputs = gaussian_with(arg_keys[0], (CLIPS, FRAMES, ROWS, COLS, D), 1.0, 6.0, ((0, 16), (1, 8)), (0, 4, 16, 2.0))
    spatial_q = draw_spatial_q(jax.random.fold_in(arg_keys[9], 71), 0)
    spatial_k = draw_spatial_k(jax.random.fold_in(arg_keys[9], 71), 0)
    spatial_v = bell_draw(arg_keys[3], (CLIPS, FRAMES, ROWS, COLS, E), 1.0, 6.0, ((0, 16), (1, 8)))
    out_weight = bell_draw(arg_keys[4], (D, E), E ** -0.5, 0.15625, ((0, 16),))
    norm_gain = jnp.clip(1.0 + 0.18 * jax.random.normal(arg_keys[5], (D,), jnp.float32), 0.1, 1.9)
    qkv_weight = draw_qkv_weight(jax.random.fold_in(arg_keys[9], 71), 0)
    grad_out = bell_draw(arg_keys[7], (CLIPS, FRAMES, ROWS, COLS, E), 1.0, 6.0, ((0, 16), (1, 8)))
    grad_resid = bell_draw(arg_keys[8], (CLIPS, FRAMES, ROWS, COLS, D), 1.0, 6.0, ((0, 16), (1, 8)))
    return dict(inputs=inputs, spatial_q=spatial_q, spatial_k=spatial_k, spatial_v=spatial_v, out_weight=out_weight, norm_gain=norm_gain, qkv_weight=qkv_weight, grad_out=grad_out, grad_resid=grad_resid)


EPSILON = 1e-06

def attend_frame(queries, key_rows, values):
    score_scale = HDIM ** (-0.5)
    scores = jnp.einsum('shd,thd->hst', queries.astype(jnp.float32), key_rows.astype(jnp.float32)) * score_scale
    row_max = lax.optimization_barrier(jnp.max(scores, axis=-1, keepdims=True))
    raised = jnp.exp(scores - row_max)
    soft_weights = raised / lax.optimization_barrier(jnp.sum(raised, axis=-1, keepdims=True))
    rounded = soft_weights.astype(jnp.bfloat16)
    mixed_heads = jnp.einsum('hst,thd->shd', rounded.astype(jnp.float32), values.astype(jnp.float32))
    return (mixed_heads.astype(jnp.bfloat16), soft_weights)

def attend_back(queries, key_rows, values, soft_weights, grad_heads):
    score_scale = HDIM ** (-0.5)
    rounded = soft_weights.astype(jnp.bfloat16).astype(jnp.float32)
    grad_wide = grad_heads.astype(jnp.float32)
    soft_grad = jnp.einsum('shd,thd->hst', grad_wide, values.astype(jnp.float32))
    dvalues = jnp.einsum('hst,shd->thd', rounded, grad_wide).astype(jnp.bfloat16)
    inner_sum = lax.optimization_barrier(jnp.sum(soft_weights * soft_grad, axis=-1, keepdims=True))
    dscores = (soft_weights * (soft_grad - inner_sum) * score_scale).astype(jnp.bfloat16).astype(jnp.float32)
    dqueries = jnp.einsum('hst,thd->shd', dscores, key_rows.astype(jnp.float32)).astype(jnp.bfloat16)
    key_grad = jnp.einsum('hst,shd->thd', dscores, queries.astype(jnp.float32)).astype(jnp.bfloat16)
    return (dqueries, key_grad, dvalues)

def reference(inputs, spatial_q, spatial_k, spatial_v, out_weight, norm_gain, qkv_weight, grad_out, grad_resid):
    clip_count = N_DP
    frame_len = ROWS * COLS
    head_width = HEADS * HDIM
    grad_scale = (clip_count * FRAMES * frame_len) ** (-0.5)

    def by_frame(array):
        return array.reshape(clip_count * FRAMES, frame_len, HEADS, HDIM)

    def spatial_step(triple):
        mixed_heads, _ = attend_frame(triple[0], triple[1], triple[2])
        return mixed_heads
    frame_q, frame_k, frame_v = (by_frame(spatial_q), by_frame(spatial_k), by_frame(spatial_v))
    mixed = lax.map(spatial_step, (frame_q, frame_k, frame_v)).reshape(-1, head_width)
    flat_in = inputs.reshape(-1, D).astype(jnp.float32)
    hidden = (flat_in + jnp.dot(mixed, out_weight.T, preferred_element_type=jnp.float32)).astype(jnp.bfloat16)
    hidden_wide = hidden.astype(jnp.float32)
    inverse = lax.rsqrt(lax.optimization_barrier(jnp.mean(hidden_wide * hidden_wide, axis=-1, keepdims=True)) + EPSILON)
    unit_rows = hidden_wide * inverse
    normed = (unit_rows * norm_gain).astype(jnp.bfloat16)
    projected = jnp.dot(normed, qkv_weight, preferred_element_type=jnp.float32).astype(jnp.bfloat16)
    token_grid = projected.reshape(clip_count, FRAMES, ROWS, COLS, HEADS, 3, HDIM)
    by_place = jnp.transpose(token_grid, (0, 2, 3, 1, 4, 5, 6)).reshape(clip_count * ROWS * COLS, FRAMES, HEADS, 3, HDIM)
    place_q, place_k, place_v = (by_place[:, :, :, 0], by_place[:, :, :, 1], by_place[:, :, :, 2])
    temporal_heads, temporal_soft = jax.vmap(attend_frame)(place_q, place_k, place_v)
    temporal_out = jnp.transpose(temporal_heads.reshape(clip_count, ROWS, COLS, FRAMES, head_width), (0, 3, 1, 2, 4))
    grad_place = jnp.transpose(grad_out, (0, 2, 3, 1, 4)).reshape(clip_count * ROWS * COLS, FRAMES, HEADS, HDIM)
    grad_queries, grad_keys, grad_values = jax.vmap(attend_back)(place_q, place_k, place_v, temporal_soft, grad_place)
    stacked = jnp.stack([grad_queries, grad_keys, grad_values], axis=3)
    stacked = stacked.reshape(clip_count, ROWS, COLS, FRAMES, 3 * head_width)
    dprojected = jnp.transpose(stacked, (0, 3, 1, 2, 4)).reshape(-1, 3 * head_width)
    qkv_grad = jnp.dot(normed.T, dprojected, preferred_element_type=jnp.float32) * grad_scale
    dnormed = jnp.dot(dprojected, qkv_weight.T, preferred_element_type=jnp.float32).astype(jnp.bfloat16)
    dnormed_wide = dnormed.astype(jnp.float32)
    gain_grad = lax.optimization_barrier(jnp.sum(dnormed_wide * unit_rows, axis=0)) * grad_scale
    scaled = dnormed_wide * norm_gain
    through_norm = inverse * (scaled - unit_rows * lax.optimization_barrier(jnp.mean(scaled * unit_rows, axis=-1, keepdims=True)))
    grad_input = (grad_resid.reshape(-1, D).astype(jnp.float32) + through_norm).astype(jnp.bfloat16)
    out_grad = jnp.dot(grad_input.T, mixed, preferred_element_type=jnp.float32) * grad_scale
    dmixed = jnp.dot(grad_input, out_weight, preferred_element_type=jnp.float32).astype(jnp.bfloat16)

    def spatial_back(frame_group):
        queries, key_rows, values, grad_heads = frame_group
        _, soft_weights = attend_frame(queries, key_rows, values)
        return attend_back(queries, key_rows, values, soft_weights, grad_heads)
    grad_sq, grad_sk, grad_sv = lax.map(spatial_back, (frame_q, frame_k, frame_v, by_frame(dmixed)))
    head_shape = (clip_count, FRAMES, ROWS, COLS, head_width)
    model_shape = (clip_count, FRAMES, ROWS, COLS, D)
    return (hidden.reshape(model_shape), temporal_out, grad_input.reshape(model_shape), grad_sq.reshape(head_shape), grad_sk.reshape(head_shape), grad_sv.reshape(head_shape), qkv_grad, out_grad, gain_grad)
```

```python
import functools

import jax
import jax.numpy as jnp
from jax import lax
from jax.experimental import pallas as pl
from jax.experimental.pallas import tpu as pltpu
from jax.sharding import PartitionSpec as P

HEADS = 24
HDIM = 64
EPSILON = 1e-06
XS = 4
SEQ = 8
DP = 16
TOK = 128
WIDTH = HEADS * HDIM
GROUP = WIDTH // SEQ
LANE = 128
BF = jnp.bfloat16
F32 = jnp.float32
SCALE = HDIM**-0.5
VMEM_LIMIT = 48 * 1024 * 1024


def params(semantics=1):
    return pltpu.CompilerParams(
        vmem_limit_bytes=VMEM_LIMIT, dimension_semantics=("arbitrary",) * semantics
    )


def dot_nt(a, b):
    return lax.dot_general(a, b, (((1,), (1,)), ((), ())), preferred_element_type=F32)


def dot_tn(a, b):
    return lax.dot_general(a, b, (((0,), (0,)), ((), ())), preferred_element_type=F32)


def dot_nn(a, b):
    return lax.dot_general(a, b, (((1,), (0,)), ((), ())), preferred_element_type=F32)


def spread(block, heads):
    lane = lax.broadcasted_iota(jnp.int32, block.shape, 1) // HDIM
    return jnp.concatenate(
        [jnp.where(lane == h, block, jnp.zeros_like(block)) for h in range(heads)], axis=0
    )


def pick(stacked, heads):
    rows = stacked.shape[0] // heads
    lane = lax.broadcasted_iota(jnp.int32, (rows, stacked.shape[1]), 1) // HDIM
    out = stacked[:rows]
    for h in range(1, heads):
        out = jnp.where(lane == h, stacked[h * rows : (h + 1) * rows], out)
    return out


def soft(scores, heads, valid=None):
    cols = scores.shape[1] // heads
    probs = []
    for h in range(heads):
        part = scores[:, h * cols : (h + 1) * cols] * SCALE
        if valid is not None:
            part = jnp.where(valid, part, -jnp.inf)
        raised = jnp.exp(part - jnp.max(part, axis=-1, keepdims=True))
        probs.append(raised / jnp.sum(raised, axis=-1, keepdims=True))
    return probs


def score_grad(probs, dprobs):
    cols = probs[0].shape[1]
    parts = []
    for h, prob in enumerate(probs):
        dpart = dprobs[:, h * cols : (h + 1) * cols]
        inner = jnp.sum(prob * dpart, axis=-1, keepdims=True)
        parts.append((prob * (dpart - inner) * SCALE).astype(BF))
    return jnp.concatenate(parts, axis=1)


def rounded(probs):
    return jnp.concatenate([p.astype(BF) for p in probs], axis=1)


PAIRS = 4


def spatial_fwd_kernel(q_ref, k_ref, v_ref, out_ref):
    for pair in range(PAIRS):
        cols = slice(pair * LANE, (pair + 1) * LANE)
        probs = soft(dot_nt(q_ref[:, cols], spread(k_ref[:, cols], 2)), 2)
        out_ref[:, cols] = dot_nn(rounded(probs), spread(v_ref[:, cols], 2)).astype(BF)


def spatial_fwd(q, k, v):
    spec = pl.BlockSpec((TOK, PAIRS * LANE), lambda i: (0, i))
    return pl.pallas_call(
        spatial_fwd_kernel,
        grid=(WIDTH // (PAIRS * LANE),),
        in_specs=[spec] * 3,
        out_specs=spec,
        out_shape=jax.ShapeDtypeStruct((TOK, WIDTH), BF),
        compiler_params=params(),
        name="spatial_fwd",
    )(q, k, v)


def spatial_bwd_kernel(gi_ref, w_ref, q_ref, k_ref, v_ref, dq_ref, dk_ref, dv_ref):
    dmixed = dot_nn(gi_ref[...], w_ref[...]).astype(BF)
    for pair in range(PAIRS):
        cols = slice(pair * LANE, (pair + 1) * LANE)
        q, dout = q_ref[:, cols], dmixed[:, cols]
        keys, values = spread(k_ref[:, cols], 2), spread(v_ref[:, cols], 2)
        probs = soft(dot_nt(q, keys), 2)
        dscores = score_grad(probs, dot_nt(dout, values))
        dv_ref[:, cols] = pick(dot_tn(rounded(probs), dout), 2).astype(BF)
        dq_ref[:, cols] = dot_nn(dscores, keys).astype(BF)
        dk_ref[:, cols] = pick(dot_tn(dscores, q), 2).astype(BF)


def spatial_bwd(grad_input, whole_out, q, k, v):
    spec = pl.BlockSpec((TOK, PAIRS * LANE), lambda i: (0, i))
    return pl.pallas_call(
        spatial_bwd_kernel,
        grid=(WIDTH // (PAIRS * LANE),),
        in_specs=[
            pl.BlockSpec((TOK, WIDTH), lambda i: (0, 0)),
            pl.BlockSpec((WIDTH, PAIRS * LANE), lambda i: (0, i)),
        ]
        + [spec] * 3,
        out_specs=[spec] * 3,
        out_shape=[jax.ShapeDtypeStruct((TOK, WIDTH), BF)] * 3,
        compiler_params=params(),
        name="spatial_bwd",
    )(grad_input, whole_out, q, k, v)


OUT_BLOCK = 512


def out_norm_kernel(mixed_ref, w_ref, in_ref, gain_ref, hidden_ref, normed_ref):
    step = pl.program_id(0)
    block = in_ref[...].astype(F32) + dot_nt(mixed_ref[...], w_ref[...])
    start = pl.multiple_of(step * OUT_BLOCK, OUT_BLOCK)
    hidden_ref[:, pl.ds(start, OUT_BLOCK)] = block.astype(BF)

    @pl.when(step == pl.num_programs(0) - 1)
    def _():
        wide = hidden_ref[...].astype(F32)
        inverse = lax.rsqrt(jnp.mean(wide * wide, axis=-1, keepdims=True) + EPSILON)
        normed_ref[...] = (wide * inverse * gain_ref[...]).astype(BF)


def out_norm(mixed, whole_out, inputs, gain):
    whole = pl.BlockSpec((TOK, WIDTH), lambda i: (0, 0))
    return pl.pallas_call(
        out_norm_kernel,
        grid=(WIDTH // OUT_BLOCK,),
        in_specs=[
            whole,
            pl.BlockSpec((OUT_BLOCK, WIDTH), lambda i: (i, 0)),
            pl.BlockSpec((TOK, OUT_BLOCK), lambda i: (0, i)),
            pl.BlockSpec((1, WIDTH), lambda i: (0, 0)),
        ],
        out_specs=[whole, whole],
        out_shape=[jax.ShapeDtypeStruct((TOK, WIDTH), BF)] * 2,
        compiler_params=params(),
        name="out_norm",
    )(mixed, whole_out, inputs, gain)


PADDED = 256
THREE = 3 * PADDED


def widen_kernel(w_ref, out_ref):
    rows = w_ref.shape[0]
    block = w_ref[...]
    for j in range(3):
        for h in range(3):
            out_ref[:, j * PADDED + h * HDIM : j * PADDED + (h + 1) * HDIM] = block[
                :, (h * 3 + j) * HDIM : (h * 3 + j + 1) * HDIM
            ]
        out_ref[:, j * PADDED + GROUP : (j + 1) * PADDED] = jnp.zeros((rows, PADDED - GROUP), BF)


def widen(head_proj):
    rows = 768
    return pl.pallas_call(
        widen_kernel,
        grid=(WIDTH // rows,),
        in_specs=[pl.BlockSpec((rows, 3 * GROUP), lambda i: (i, 0))],
        out_specs=pl.BlockSpec((rows, THREE), lambda i: (i, 0)),
        out_shape=jax.ShapeDtypeStruct((WIDTH, THREE), BF),
        compiler_params=params(),
        name="widen",
    )(head_proj)


POS = 16


def temporal_kernel(order_ref, *refs):
    proj, (grad_ref, out_ref, dproj_ref) = refs[:SEQ], refs[SEQ:]

    def rows(j):
        return jnp.concatenate(
            [p[:, j * PADDED : j * PADDED + GROUP] for p in proj], axis=0
        )

    q = rows(0)
    keys, values = spread(rows(1), 3), spread(rows(2), 3)
    dout = jnp.concatenate([grad_ref[order_ref[r]] for r in range(SEQ)], axis=0)
    shape = (SEQ * POS, SEQ * POS)
    valid = (
        lax.broadcasted_iota(jnp.int32, shape, 0) % POS
        == lax.broadcasted_iota(jnp.int32, shape, 1) % POS
    )
    probs = soft(dot_nt(q, keys), 3, valid)
    prob_round = rounded(probs)
    heads_out = dot_nn(prob_round, values).astype(BF)
    dscores = score_grad(probs, dot_nt(dout, values))
    grads = (
        dot_nn(dscores, keys).astype(BF),
        pick(dot_tn(dscores, q), 3).astype(BF),
        pick(dot_tn(prob_round, dout), 3).astype(BF),
    )
    for r in range(SEQ):
        here = slice(r * POS, (r + 1) * POS)
        out_ref[order_ref[r]] = heads_out[here]
        for j in range(3):
            dproj_ref[r, :, j * PADDED : j * PADDED + GROUP] = grads[j][here]
            dproj_ref[r, :, j * PADDED + GROUP : (j + 1) * PADDED] = jnp.zeros(
                (POS, PADDED - GROUP), BF
            )


def temporal(order, proj, grad_heads):
    frame = pl.BlockSpec((POS, THREE), lambda i, o: (i, 0))
    heads = pl.BlockSpec((SEQ, POS, GROUP), lambda i, o: (0, i, 0))
    return pl.pallas_call(
        temporal_kernel,
        grid_spec=pltpu.PrefetchScalarGridSpec(
            num_scalar_prefetch=1,
            grid=(TOK // POS,),
            in_specs=[frame] * SEQ + [heads],
            out_specs=[heads, pl.BlockSpec((SEQ, POS, THREE), lambda i, o: (0, i, 0))],
        ),
        out_shape=[
            jax.ShapeDtypeStruct((SEQ, TOK, GROUP), BF),
            jax.ShapeDtypeStruct((SEQ, TOK, THREE), BF),
        ],
        compiler_params=params(),
        name="temporal",
    )(order, *proj, grad_heads)


GRAD_ROWS = 512


def qkv_grad_kernel(factor, *refs):
    frames, dproj_ref, out_ref = refs[:-2], refs[-2], refs[-1]
    left = jnp.concatenate([f[...] for f in frames], axis=0)
    right = dproj_ref[...].reshape(SEQ * TOK, THREE)
    full = (dot_tn(left, right) * factor).astype(BF)
    for j in range(3):
        for h in range(3):
            out_ref[:, (h * 3 + j) * HDIM : (h * 3 + j + 1) * HDIM] = full[
                :, j * PADDED + h * HDIM : j * PADDED + (h + 1) * HDIM
            ]


def qkv_product(frames, dproj, factor):
    return pl.pallas_call(
        functools.partial(qkv_grad_kernel, factor),
        grid=(WIDTH // GRAD_ROWS,),
        in_specs=[pl.BlockSpec((f.shape[0], GRAD_ROWS), lambda i: (0, i)) for f in frames]
        + [pl.BlockSpec((SEQ, TOK, THREE), lambda i: (0, 0, 0))],
        out_specs=pl.BlockSpec((GRAD_ROWS, 3 * GROUP), lambda i: (i, 0)),
        out_shape=jax.ShapeDtypeStruct((WIDTH, 3 * GROUP), BF),
        compiler_params=params(),
        name="qkv_product",
    )(*frames, dproj)


SHARE = 12
SLOT = 16
FOUR = 4


def grad_input_kernel(factor, sum_a, sum_b, sum_c, sum_d, hidden_ref, resid_ref, gain_ref,
                      out_ref, groups_ref, gain_out_ref):
    def wide(ref):
        return ref[...].astype(F32)

    dnormed = (wide(sum_a) + wide(sum_b) + wide(sum_c) + wide(sum_d)).astype(BF).astype(F32)
    hidden = wide(hidden_ref)
    inverse = lax.rsqrt(jnp.mean(hidden * hidden, axis=-1, keepdims=True) + EPSILON)
    unit = hidden * inverse
    gain_out_ref[...] = jnp.sum(dnormed * unit, axis=0, keepdims=True) * factor
    scaled = dnormed * gain_ref[...]
    through = inverse * (scaled - unit * jnp.mean(scaled * unit, axis=-1, keepdims=True))
    grad = (wide(resid_ref) + through).astype(BF)
    out_ref[...] = grad
    rows, cols = FOUR * SHARE * SEQ, FOUR * SLOT * SEQ
    source = lax.broadcasted_iota(jnp.int32, (rows, cols), 0)
    target = lax.broadcasted_iota(jnp.int32, (rows, cols), 1)
    group = target // (FOUR * SLOT)
    block = (target // SLOT) % FOUR
    turn = target % SLOT
    wanted = block * (SHARE * SEQ) + group * SHARE + turn
    move = jnp.where((source == wanted) & (turn < SHARE), 1.0, 0.0).astype(BF)
    for four in range(DP // FOUR):
        moved = dot_nn(grad[:, four * rows : (four + 1) * rows], move).astype(BF)
        for j in range(SEQ):
            groups_ref[j, :, four * FOUR * SLOT : (four + 1) * FOUR * SLOT] = moved[
                :, j * FOUR * SLOT : (j + 1) * FOUR * SLOT
            ]


def grad_input_call(sums, hidden, resid, gain, factor):
    return pl.pallas_call(
        functools.partial(grad_input_kernel, factor),
        out_shape=[
            jax.ShapeDtypeStruct((TOK, WIDTH), BF),
            jax.ShapeDtypeStruct((SEQ, TOK, DP * SLOT), BF),
            jax.ShapeDtypeStruct((1, WIDTH), F32),
        ],
        compiler_params=pltpu.CompilerParams(vmem_limit_bytes=VMEM_LIMIT),
        name="grad_input",
    )(*sums, hidden, resid, gain)


def out_product_kernel(factor, order_ref, groups_ref, *refs):
    frames, out_ref = refs[:-1], refs[-1]
    left = jnp.concatenate([groups_ref[order_ref[r]] for r in range(SEQ)], axis=0)
    right = jnp.concatenate([f[...] for f in frames], axis=0)
    out_ref[...] = (dot_tn(left, right) * factor).astype(BF)


def out_product(order, groups, frames, factor):
    cols = 512
    return pl.pallas_call(
        functools.partial(out_product_kernel, factor),
        grid_spec=pltpu.PrefetchScalarGridSpec(
            num_scalar_prefetch=1,
            grid=(WIDTH // cols,),
            in_specs=[pl.BlockSpec((SEQ, TOK, DP * SLOT), lambda i, o: (0, 0, 0))]
            + [pl.BlockSpec((f.shape[0], cols), lambda i, o: (0, i)) for f in frames],
            out_specs=pl.BlockSpec((DP * SLOT, cols), lambda i, o: (0, i)),
        ),
        out_shape=jax.ShapeDtypeStruct((DP * SLOT, WIDTH), BF),
        compiler_params=params(),
        name="out_product",
    )(order, groups, *frames)


def along_x(array, shift):
    pairs = [(i, ((i // 2 + shift) % XS) * 2 + i % 2) for i in range(SEQ)]
    return lax.ppermute(array, "seq", pairs)


def across_y(array):
    return lax.ppermute(array, "seq", [(i, i ^ 1) for i in range(SEQ)])


HALF = TOK // 2


def gather_frames(own):
    behind, ahead, partner = along_x(own, 1), along_x(own, -1), across_y(own)
    far_top, far_low = along_x(behind[:HALF], 1), along_x(ahead[HALF:], -1)
    partner_behind, partner_ahead = along_x(partner, 1), along_x(partner, -1)
    return (
        own, behind, ahead, far_top, far_low,
        partner, partner_behind, partner_ahead, across_y(far_top), across_y(far_low),
    )


def whole_frames(parts):
    own, behind, ahead, top, low, partner, pbehind, pahead, ptop, plow = parts
    return (
        own, behind, ahead, jnp.concatenate([top, low], axis=0),
        partner, pbehind, pahead, jnp.concatenate([ptop, plow], axis=0),
    )


def scatter_frames(shares):
    own, behind, ahead, far, partner, pbehind, pahead, pfar = shares
    far = far + across_y(pfar)
    partner = partner + along_x(pbehind, -1) + along_x(pahead, 1)
    top, low = along_x(far[:HALF], -1), along_x(far[HALF:], 1)
    behind = jnp.concatenate([behind[:HALF] + top, behind[HALF:]], axis=0)
    ahead = jnp.concatenate([ahead[:HALF], ahead[HALF:] + low], axis=0)
    return own, across_y(partner), along_x(behind, -1), along_x(ahead, 1)


def body(
    inputs, spatial_q, spatial_k, spatial_v, out_weight, norm_gain, qkv_weight, grad_out, grad_resid
):
    block_shape = inputs.shape
    factor = (TOK * DP * SEQ) ** (-0.5)
    flat_in, q, k, v, dout, resid = (
        a.reshape(TOK, WIDTH)
        for a in (inputs, spatial_q, spatial_k, spatial_v, grad_out, grad_resid)
    )
    gain = norm_gain.reshape(1, WIDTH)
    me = lax.axis_index("seq")
    place_x, place_y = me // 2, me % 2
    order = jnp.stack(
        [((place_x + s) % XS) * 2 + y for y in (place_y, 1 - place_y) for s in (0, 3, 1, 2)]
    ).astype(jnp.int32)

    whole_out = lax.all_gather(out_weight, "dp", axis=0, tiled=True)
    head_proj = lax.all_gather(qkv_weight, "dp", axis=0, tiled=True)

    grad_heads = lax.all_to_all(
        dout.reshape(TOK, SEQ, GROUP).transpose(1, 0, 2), "seq", 0, 0, tiled=True
    )
    mixed = spatial_fwd(q, k, v)
    mixed_parts = gather_frames(mixed)
    hidden, normed = out_norm(mixed, whole_out, flat_in, gain)
    normed_parts = gather_frames(normed)
    wide_proj = widen(head_proj)
    proj = [dot_nn(f, wide_proj).astype(BF) for f in whole_frames(normed_parts)]
    heads_out, dproj = temporal(order, proj, grad_heads)
    shares = [dot_nt(dproj[r], wide_proj).astype(BF) for r in range(SEQ)]
    sums = scatter_frames(shares)
    qkv_share = qkv_product(normed_parts, dproj, factor)
    qkv_grad = lax.psum_scatter(qkv_share, "dp", scatter_dimension=0, tiled=True).astype(F32)
    temporal_out = lax.all_to_all(heads_out, "seq", 0, 0, tiled=True)
    temporal_out = temporal_out.transpose(1, 0, 2).reshape(TOK, WIDTH)

    grad_input, groups, local_gain = grad_input_call(sums, hidden, resid, gain, factor)
    gain_grad = lax.psum(local_gain.reshape(WIDTH), ("dp", "seq"))
    groups = lax.all_to_all(groups, "seq", 0, 0, tiled=True)
    out_share = out_product(order, groups, mixed_parts, factor)
    out_rows = lax.psum_scatter(out_share, "dp", scatter_dimension=0, tiled=True)
    out_all = lax.all_to_all(
        jnp.broadcast_to(out_rows[None], (SEQ, SLOT, WIDTH)), "seq", 0, 0, tiled=True
    )
    out_grad = out_all[:, :SHARE].reshape(SEQ * SHARE, WIDTH).astype(F32)
    grad_q, grad_k, grad_v = spatial_bwd(grad_input, whole_out, q, k, v)
    return tuple(
        a.reshape(block_shape) for a in (hidden, temporal_out, grad_input, grad_q, grad_k, grad_v)
    ) + (qkv_grad, out_grad, gain_grad)


def solution(mesh):
    tokens = P("dp", "seq", None, None, None)
    return jax.shard_map(
        body,
        mesh=mesh,
        in_specs=(
            tokens, tokens, tokens, tokens, P("dp", None), P(), P("dp", "seq"), tokens, tokens,
        ),
        out_specs=(
            tokens, tokens, tokens, tokens, tokens, tokens, P("dp", "seq"), P("dp", None), P(),
        ),
        check_vma=False,
    )
```

```python
import functools

import jax
import jax.numpy as jnp
from jax import lax
from jax.experimental import pallas as pl
from jax.experimental.pallas import tpu as pltpu
from jax.sharding import PartitionSpec as P

HEADS = 24
HDIM = 64
EPSILON = 1e-06
XS = 4
SEQ = 8
DP = 16
TOK = 128
WIDTH = HEADS * HDIM
GROUP = WIDTH // SEQ
LANE = 128
BF = jnp.bfloat16
F32 = jnp.float32
SCALE = HDIM**-0.5
VMEM_LIMIT = 24 * 1024 * 1024
HBM_RATE = 3_000_000


def params():
    return pltpu.CompilerParams(vmem_limit_bytes=VMEM_LIMIT)


def cost(micros):
    return pl.CostEstimate(flops=0, bytes_accessed=int(micros * HBM_RATE), transcendentals=0)


def dot_nt(a, b):
    return lax.dot_general(a, b, (((1,), (1,)), ((), ())), preferred_element_type=F32)


def dot_tn(a, b):
    return lax.dot_general(a, b, (((0,), (0,)), ((), ())), preferred_element_type=F32)


def dot_nn(a, b):
    return lax.dot_general(a, b, (((1,), (0,)), ((), ())), preferred_element_type=F32)


def spread(block, heads):
    lane = lax.broadcasted_iota(jnp.int32, block.shape, 1) // HDIM
    return jnp.concatenate(
        [jnp.where(lane == h, block, jnp.zeros_like(block)) for h in range(heads)], axis=0
    )


def pick(stacked, heads):
    rows = stacked.shape[0] // heads
    lane = lax.broadcasted_iota(jnp.int32, (rows, stacked.shape[1]), 1) // HDIM
    out = stacked[:rows]
    for h in range(1, heads):
        out = jnp.where(lane == h, stacked[h * rows : (h + 1) * rows], out)
    return out


def soft(scores, heads, valid=None):
    cols = scores.shape[1] // heads
    probs = []
    for h in range(heads):
        part = scores[:, h * cols : (h + 1) * cols] * SCALE
        if valid is not None:
            part = jnp.where(valid, part, -jnp.inf)
        raised = jnp.exp(part - jnp.max(part, axis=-1, keepdims=True))
        probs.append(raised / jnp.sum(raised, axis=-1, keepdims=True))
    return probs


def score_grad(probs, dprobs):
    cols = probs[0].shape[1]
    parts = []
    for h, prob in enumerate(probs):
        dpart = dprobs[:, h * cols : (h + 1) * cols]
        inner = jnp.sum(prob * dpart, axis=-1, keepdims=True)
        parts.append((prob * (dpart - inner) * SCALE).astype(BF))
    return jnp.concatenate(parts, axis=1)


def rounded(probs):
    return jnp.concatenate([p.astype(BF) for p in probs], axis=1)


PAIRS = 4


def spatial_fwd_kernel(q_ref, k_ref, v_ref, out_ref):
    for pair in range(PAIRS):
        cols = slice(pair * LANE, (pair + 1) * LANE)
        probs = soft(dot_nt(q_ref[:, cols], spread(k_ref[:, cols], 2)), 2)
        out_ref[:, cols] = dot_nn(rounded(probs), spread(v_ref[:, cols], 2)).astype(BF)


def spatial_fwd(q, k, v):
    spec = pl.BlockSpec((TOK, PAIRS * LANE), lambda i: (0, i))
    return pl.pallas_call(
        spatial_fwd_kernel,
        grid=(WIDTH // (PAIRS * LANE),),
        in_specs=[spec] * 3,
        out_specs=spec,
        out_shape=jax.ShapeDtypeStruct((TOK, WIDTH), BF),
        compiler_params=params(),
        name="spatial_fwd",
        cost_estimate=cost(4),
    )(q, k, v)


def spatial_bwd_kernel(gi_ref, w_ref, q_ref, k_ref, v_ref, dq_ref, dk_ref, dv_ref):
    dmixed = dot_nn(gi_ref[...], w_ref[...]).astype(BF)
    for pair in range(PAIRS):
        cols = slice(pair * LANE, (pair + 1) * LANE)
        q, dout = q_ref[:, cols], dmixed[:, cols]
        keys, values = spread(k_ref[:, cols], 2), spread(v_ref[:, cols], 2)
        probs = soft(dot_nt(q, keys), 2)
        dscores = score_grad(probs, dot_nt(dout, values))
        dv_ref[:, cols] = pick(dot_tn(rounded(probs), dout), 2).astype(BF)
        dq_ref[:, cols] = dot_nn(dscores, keys).astype(BF)
        dk_ref[:, cols] = pick(dot_tn(dscores, q), 2).astype(BF)


def spatial_bwd(grad_input, whole_out, q, k, v):
    spec = pl.BlockSpec((TOK, PAIRS * LANE), lambda i: (0, i))
    return pl.pallas_call(
        spatial_bwd_kernel,
        grid=(WIDTH // (PAIRS * LANE),),
        in_specs=[
            pl.BlockSpec((TOK, WIDTH), lambda i: (0, 0)),
            pl.BlockSpec((WIDTH, PAIRS * LANE), lambda i: (0, i)),
        ]
        + [spec] * 3,
        out_specs=[spec] * 3,
        out_shape=[jax.ShapeDtypeStruct((TOK, WIDTH), BF)] * 3,
        compiler_params=params(),
        name="spatial_bwd",
        cost_estimate=cost(9),
    )(grad_input, whole_out, q, k, v)


OUT_BLOCK = 512


def out_norm_kernel(mixed_ref, w_ref, in_ref, gain_ref, hidden_ref, normed_ref):
    step = pl.program_id(0)
    block = in_ref[...].astype(F32) + dot_nt(mixed_ref[...], w_ref[...])
    start = pl.multiple_of(step * OUT_BLOCK, OUT_BLOCK)
    hidden_ref[:, pl.ds(start, OUT_BLOCK)] = block.astype(BF)

    @pl.when(step == pl.num_programs(0) - 1)
    def _():
        wide = hidden_ref[...].astype(F32)
        inverse = lax.rsqrt(jnp.mean(wide * wide, axis=-1, keepdims=True) + EPSILON)
        normed_ref[...] = (wide * inverse * gain_ref[...]).astype(BF)


def out_norm(mixed, whole_out, inputs, gain):
    whole = pl.BlockSpec((TOK, WIDTH), lambda i: (0, 0))
    return pl.pallas_call(
        out_norm_kernel,
        grid=(WIDTH // OUT_BLOCK,),
        in_specs=[
            whole,
            pl.BlockSpec((OUT_BLOCK, WIDTH), lambda i: (i, 0)),
            pl.BlockSpec((TOK, OUT_BLOCK), lambda i: (0, i)),
            pl.BlockSpec((1, WIDTH), lambda i: (0, 0)),
        ],
        out_specs=[whole, whole],
        out_shape=[jax.ShapeDtypeStruct((TOK, WIDTH), BF)] * 2,
        compiler_params=params(),
        name="out_norm",
        cost_estimate=cost(4),
    )(mixed, whole_out, inputs, gain)


PADDED = 256
THREE = 3 * PADDED


def widen_kernel(w_ref, out_ref):
    rows = w_ref.shape[0]
    block = w_ref[...]
    for j in range(3):
        for h in range(3):
            out_ref[:, j * PADDED + h * HDIM : j * PADDED + (h + 1) * HDIM] = block[
                :, (h * 3 + j) * HDIM : (h * 3 + j + 1) * HDIM
            ]
        out_ref[:, j * PADDED + GROUP : (j + 1) * PADDED] = jnp.zeros((rows, PADDED - GROUP), BF)


def widen(head_proj):
    rows = 768
    return pl.pallas_call(
        widen_kernel,
        grid=(WIDTH // rows,),
        in_specs=[pl.BlockSpec((rows, 3 * GROUP), lambda i: (i, 0))],
        out_specs=pl.BlockSpec((rows, THREE), lambda i: (i, 0)),
        out_shape=jax.ShapeDtypeStruct((WIDTH, THREE), BF),
        compiler_params=params(),
        name="widen",
        cost_estimate=cost(1.5),
    )(head_proj)


POS = 16


def temporal_kernel(order_ref, *refs):
    proj, (grad_ref, out_ref, dproj_ref) = refs[:SEQ], refs[SEQ:]

    def rows(j):
        return jnp.concatenate(
            [p[:, j * PADDED : j * PADDED + GROUP] for p in proj], axis=0
        )

    q = rows(0)
    keys, values = spread(rows(1), 3), spread(rows(2), 3)
    dout = jnp.concatenate([grad_ref[order_ref[r]] for r in range(SEQ)], axis=0)
    shape = (SEQ * POS, SEQ * POS)
    valid = (
        lax.broadcasted_iota(jnp.int32, shape, 0) % POS
        == lax.broadcasted_iota(jnp.int32, shape, 1) % POS
    )
    probs = soft(dot_nt(q, keys), 3, valid)
    prob_round = rounded(probs)
    heads_out = dot_nn(prob_round, values).astype(BF)
    dscores = score_grad(probs, dot_nt(dout, values))
    grads = (
        dot_nn(dscores, keys).astype(BF),
        pick(dot_tn(dscores, q), 3).astype(BF),
        pick(dot_tn(prob_round, dout), 3).astype(BF),
    )
    for r in range(SEQ):
        here = slice(r * POS, (r + 1) * POS)
        out_ref[order_ref[r]] = heads_out[here]
        for j in range(3):
            dproj_ref[r, :, j * PADDED : j * PADDED + GROUP] = grads[j][here]
            dproj_ref[r, :, j * PADDED + GROUP : (j + 1) * PADDED] = jnp.zeros(
                (POS, PADDED - GROUP), BF
            )


def temporal(order, proj, grad_heads):
    frame = pl.BlockSpec((POS, THREE), lambda i, o: (i, 0))
    heads = pl.BlockSpec((SEQ, POS, GROUP), lambda i, o: (0, i, 0))
    return pl.pallas_call(
        temporal_kernel,
        grid_spec=pltpu.PrefetchScalarGridSpec(
            num_scalar_prefetch=1,
            grid=(TOK // POS,),
            in_specs=[frame] * SEQ + [heads],
            out_specs=[heads, pl.BlockSpec((SEQ, POS, THREE), lambda i, o: (0, i, 0))],
        ),
        out_shape=[
            jax.ShapeDtypeStruct((SEQ, TOK, GROUP), BF),
            jax.ShapeDtypeStruct((SEQ, TOK, THREE), BF),
        ],
        compiler_params=params(),
        name="temporal",
        cost_estimate=cost(9),
    )(order, *proj, grad_heads)


GRAD_ROWS = 512


def qkv_grad_kernel(factor, *refs):
    frames, dproj_ref, out_ref = refs[:-2], refs[-2], refs[-1]
    left = jnp.concatenate([f[...] for f in frames], axis=0)
    right = dproj_ref[...].reshape(SEQ * TOK, THREE)
    full = (dot_tn(left, right) * factor).astype(BF)
    for j in range(3):
        for h in range(3):
            out_ref[:, (h * 3 + j) * HDIM : (h * 3 + j + 1) * HDIM] = full[
                :, j * PADDED + h * HDIM : j * PADDED + (h + 1) * HDIM
            ]


def qkv_product(frames, dproj, factor):
    return pl.pallas_call(
        functools.partial(qkv_grad_kernel, factor),
        grid=(WIDTH // GRAD_ROWS,),
        in_specs=[pl.BlockSpec((f.shape[0], GRAD_ROWS), lambda i: (0, i)) for f in frames]
        + [pl.BlockSpec((SEQ, TOK, THREE), lambda i: (0, 0, 0))],
        out_specs=pl.BlockSpec((GRAD_ROWS, 3 * GROUP), lambda i: (i, 0)),
        out_shape=jax.ShapeDtypeStruct((WIDTH, 3 * GROUP), BF),
        compiler_params=params(),
        name="qkv_product",
        cost_estimate=cost(5),
    )(*frames, dproj)


SHARE = 12
SLOT = 16
FOUR = 4
EXTRA = 16
GROUPED = DP * SLOT


def mover():
    shape = (FOUR * SHARE * SEQ, FOUR * SLOT * SEQ)
    source = lax.broadcasted_iota(jnp.int32, shape, 0)
    target = lax.broadcasted_iota(jnp.int32, shape, 1)
    group = target // (FOUR * SLOT)
    block = (target // SLOT) % FOUR
    turn = target % SLOT
    wanted = block * (SHARE * SEQ) + group * SHARE + turn
    return jnp.where((source == wanted) & (turn < SHARE), 1.0, 0.0).astype(BF)


def two_parts(row):
    high = row.astype(BF)
    return high, (row - high.astype(F32)).astype(BF)


def grad_input_kernel(factor, sum_a, sum_b, sum_c, sum_d, hidden_ref, resid_ref, gain_ref,
                      out_ref, groups_ref):
    def wide(ref):
        return ref[...].astype(F32)

    dnormed = (wide(sum_a) + wide(sum_b) + wide(sum_c) + wide(sum_d)).astype(BF).astype(F32)
    hidden = wide(hidden_ref)
    inverse = lax.rsqrt(jnp.mean(hidden * hidden, axis=-1, keepdims=True) + EPSILON)
    unit = hidden * inverse
    gain_high, gain_low = two_parts(jnp.sum(dnormed * unit, axis=0, keepdims=True) * factor)
    scaled = dnormed * gain_ref[...]
    through = inverse * (scaled - unit * jnp.mean(scaled * unit, axis=-1, keepdims=True))
    grad = (wide(resid_ref) + through).astype(BF)
    out_ref[...] = grad
    row = lax.broadcasted_iota(jnp.int32, (EXTRA, WIDTH), 0)
    extra = jnp.where(row == 0, gain_high.astype(F32), jnp.where(row == 1, gain_low.astype(F32), 0.0))
    both = jnp.concatenate([grad, extra.astype(BF)], axis=0)
    move = mover()
    rows, cols = FOUR * SHARE * SEQ, FOUR * SLOT
    for four in range(DP // FOUR):
        moved = dot_nn(both[:, four * rows : (four + 1) * rows], move).astype(BF)
        for j in range(SEQ):
            groups_ref[j, :, four * cols : (four + 1) * cols] = moved[:, j * cols : (j + 1) * cols]


def grad_input_call(sums, hidden, resid, gain, factor):
    return pl.pallas_call(
        functools.partial(grad_input_kernel, factor),
        out_shape=[
            jax.ShapeDtypeStruct((TOK, WIDTH), BF),
            jax.ShapeDtypeStruct((SEQ, TOK + EXTRA, GROUPED), BF),
        ],
        compiler_params=params(),
        name="grad_input",
        cost_estimate=cost(2),
    )(*sums, hidden, resid, gain)


def out_product_kernel(factor, order_ref, groups_ref, *refs):
    frames, out_ref = refs[:-1], refs[-1]
    cols = out_ref.shape[1]
    left = jnp.concatenate([groups_ref[order_ref[r], :TOK] for r in range(SEQ)], axis=0)
    right = jnp.concatenate([f[...] for f in frames], axis=0)
    product = dot_tn(left, right) * factor
    extras = sum(groups_ref[r, TOK:].astype(F32) for r in range(SEQ))
    high, low = two_parts(extras[0:1] + extras[1:2])
    filler = jnp.zeros((1, cols - GROUPED), F32)
    turn = lax.broadcasted_iota(jnp.int32, product.shape, 0) % SLOT
    first = pl.program_id(0) == 0
    for place, part in ((SHARE, high), (SHARE + 1, low)):
        full = jnp.concatenate([part.astype(F32), filler], axis=1)
        product = jnp.where((turn == place) & first, full, product)
    out_ref[...] = product.astype(BF)


def out_product(order, groups, frames, factor):
    cols = 512
    return pl.pallas_call(
        functools.partial(out_product_kernel, factor),
        grid_spec=pltpu.PrefetchScalarGridSpec(
            num_scalar_prefetch=1,
            grid=(WIDTH // cols,),
            in_specs=[pl.BlockSpec((SEQ, TOK + EXTRA, GROUPED), lambda i, o: (0, 0, 0))]
            + [pl.BlockSpec((f.shape[0], cols), lambda i, o: (0, i)) for f in frames],
            out_specs=pl.BlockSpec((GROUPED, cols), lambda i, o: (0, i)),
        ),
        out_shape=jax.ShapeDtypeStruct((GROUPED, WIDTH), BF),
        compiler_params=params(),
        name="out_product",
        cost_estimate=cost(5),
    )(order, groups, *frames)


def fold_kernel(in_ref, out_ref):
    total = in_ref[0].astype(F32)
    for d in range(1, DP // 2):
        total = total + in_ref[d].astype(F32)
    high, low = two_parts(total[SHARE : SHARE + 1] + total[SHARE + 1 : SHARE + 2])
    turn = lax.broadcasted_iota(jnp.int32, total.shape, 0)
    total = jnp.where(turn == SHARE, high.astype(F32), total)
    total = jnp.where(turn == SHARE + 1, low.astype(F32), total).astype(BF)
    for j in range(SEQ):
        out_ref[j] = total


def fold(pieces):
    return pl.pallas_call(
        fold_kernel,
        out_shape=jax.ShapeDtypeStruct((SEQ, SLOT, WIDTH), BF),
        compiler_params=params(),
        name="fold",
        cost_estimate=cost(1.5),
    )(pieces)


def finish_kernel(in_ref, out_ref, gain_ref):
    out_ref[...] = jnp.concatenate(
        [in_ref[j].astype(F32)[:SHARE] for j in range(SEQ)], axis=0
    )
    move = mover()
    rows, cols = FOUR * SHARE * SEQ, FOUR * SLOT
    for four in range(DP // FOUR):
        left = jnp.concatenate(
            [in_ref[j, :, four * cols : (four + 1) * cols] for j in range(SEQ)], axis=1
        )
        back = dot_nt(left, move)
        gain_ref[:, four * rows : (four + 1) * rows] = (
            back[SHARE : SHARE + 1] + back[SHARE + 1 : SHARE + 2]
        )


def finish(gathered):
    return pl.pallas_call(
        finish_kernel,
        out_shape=[
            jax.ShapeDtypeStruct((SEQ * SHARE, WIDTH), F32),
            jax.ShapeDtypeStruct((1, WIDTH), F32),
        ],
        compiler_params=params(),
        name="finish",
        cost_estimate=cost(2),
    )(gathered)


def along_x(array, shift):
    pairs = [(i, ((i // 2 + shift) % XS) * 2 + i % 2) for i in range(SEQ)]
    return lax.ppermute(array, "seq", pairs)


def across_y(array):
    return lax.ppermute(array, "seq", [(i, i ^ 1) for i in range(SEQ)])


HALF = TOK // 2


def gather_frames(own):
    behind, ahead, partner = along_x(own, 1), along_x(own, -1), across_y(own)
    far_top, far_low = along_x(behind[:HALF], 1), along_x(ahead[HALF:], -1)
    partner_behind, partner_ahead = along_x(partner, 1), along_x(partner, -1)
    return (
        own, behind, ahead, far_top, far_low,
        partner, partner_behind, partner_ahead, across_y(far_top), across_y(far_low),
    )


def whole_frames(parts):
    own, behind, ahead, top, low, partner, pbehind, pahead, ptop, plow = parts
    return (
        own, behind, ahead, jnp.concatenate([top, low], axis=0),
        partner, pbehind, pahead, jnp.concatenate([ptop, plow], axis=0),
    )


def scatter_frames(shares):
    own, behind, ahead, far, partner, pbehind, pahead, pfar = shares
    far = far + across_y(pfar)
    partner = partner + along_x(pbehind, -1) + along_x(pahead, 1)
    top, low = along_x(far[:HALF], -1), along_x(far[HALF:], 1)
    behind = jnp.concatenate([behind[:HALF] + top, behind[HALF:]], axis=0)
    ahead = jnp.concatenate([ahead[:HALF], ahead[HALF:] + low], axis=0)
    return own, across_y(partner), along_x(behind, -1), along_x(ahead, 1)


def dp_pieces(share):
    blocks = share.reshape(DP // 2, 2, SLOT, WIDTH)
    core = lax.axis_index("dp") % 2
    mine = lax.dynamic_index_in_dim(blocks, core, 1, keepdims=False)
    other = lax.dynamic_index_in_dim(blocks, 1 - core, 1, keepdims=False)
    got = lax.ppermute(other, "dp", [(i, i ^ 1) for i in range(DP)])
    groups = [[2 * i + c for i in range(DP // 2)] for c in range(2)]
    return lax.all_to_all(mine + got, "dp", 0, 0, axis_index_groups=groups, tiled=True)


def body(
    inputs, spatial_q, spatial_k, spatial_v, out_weight, norm_gain, qkv_weight, grad_out, grad_resid
):
    block_shape = inputs.shape
    factor = (TOK * DP * SEQ) ** (-0.5)
    flat_in, q, k, v, dout, resid = (
        a.reshape(TOK, WIDTH)
        for a in (inputs, spatial_q, spatial_k, spatial_v, grad_out, grad_resid)
    )
    gain = norm_gain.reshape(1, WIDTH)
    me = lax.axis_index("seq")
    place_x, place_y = me // 2, me % 2
    order = jnp.stack(
        [((place_x + s) % XS) * 2 + y for y in (place_y, 1 - place_y) for s in (0, 3, 1, 2)]
    ).astype(jnp.int32)

    whole_out = lax.all_gather(out_weight, "dp", axis=0, tiled=True)
    head_proj = lax.all_gather(qkv_weight, "dp", axis=0, tiled=True)

    mixed = spatial_fwd(q, k, v)
    grad_heads = lax.all_to_all(
        dout.reshape(TOK, SEQ, GROUP).transpose(1, 0, 2), "seq", 0, 0, tiled=True
    )
    mixed_parts = gather_frames(mixed)
    whole_out, grad_heads, *mixed_parts = lax.optimization_barrier(
        (whole_out, grad_heads, *mixed_parts)
    )
    hidden, normed = out_norm(mixed, whole_out, flat_in, gain)
    normed_parts = gather_frames(normed)
    head_proj, *early = lax.optimization_barrier((head_proj, *normed_parts[:8]))
    wide_proj = widen(head_proj)
    proj = [
        dot_nn(f, wide_proj).astype(BF) for f in whole_frames((*early, *normed_parts[8:]))
    ]
    heads_out, dproj = temporal(order, proj, grad_heads)
    shares = [dot_nt(dproj[r], wide_proj).astype(BF) for r in range(SEQ)]
    *shares, dproj, heads_out = lax.optimization_barrier((*shares, dproj, heads_out))
    qkv_share = qkv_product(normed_parts, dproj, factor)
    sums = scatter_frames(shares)
    *sums, qkv_share = lax.optimization_barrier((*sums, qkv_share))
    qkv_grad = lax.psum_scatter(qkv_share, "dp", scatter_dimension=0, tiled=True).astype(F32)

    grad_input, groups = grad_input_call(sums, hidden, resid, gain, factor)
    groups = lax.all_to_all(groups, "seq", 0, 0, tiled=True)
    out_share = out_product(order, groups, mixed_parts, factor)
    pieces = dp_pieces(out_share)
    temporal_out = lax.all_to_all(heads_out, "seq", 0, 0, tiled=True)
    temporal_out = temporal_out.transpose(1, 0, 2).reshape(TOK, WIDTH)
    grad_q, grad_k, grad_v = spatial_bwd(grad_input, whole_out, q, k, v)
    out_grad, gain_grad = finish(lax.all_to_all(fold(pieces), "seq", 0, 0, tiled=True))
    return tuple(
        a.reshape(block_shape) for a in (hidden, temporal_out, grad_input, grad_q, grad_k, grad_v)
    ) + (qkv_grad, out_grad, gain_grad.reshape(WIDTH))


def solution(mesh):
    tokens = P("dp", "seq", None, None, None)
    return jax.shard_map(
        body,
        mesh=mesh,
        in_specs=(
            tokens, tokens, tokens, tokens, P("dp", None), P(), P("dp", "seq"), tokens, tokens,
        ),
        out_specs=(
            tokens, tokens, tokens, tokens, tokens, tokens, P("dp", "seq"), P("dp", None), P(),
        ),
        check_vma=False,
    )
```

```python
import functools

import jax
import jax.numpy as jnp
from jax import lax
from jax.experimental import pallas as pl
from jax.experimental.pallas import tpu as pltpu
from jax.sharding import PartitionSpec as P

HEADS = 24
HDIM = 64
EPSILON = 1e-06
XS = 4
SEQ = 8
DP = 16
TOK = 128
WIDTH = HEADS * HDIM
GROUP = WIDTH // SEQ
LANE = 128
BF = jnp.bfloat16
F32 = jnp.float32
SCALE = HDIM**-0.5
VMEM_LIMIT = 20 * 1024 * 1024
HBM_RATE = 3_000_000


def params(limit=VMEM_LIMIT):
    return pltpu.CompilerParams(vmem_limit_bytes=limit)


def cost(micros):
    return pl.CostEstimate(flops=0, bytes_accessed=int(micros * HBM_RATE), transcendentals=0)


def dot_nt(a, b):
    return lax.dot_general(a, b, (((1,), (1,)), ((), ())), preferred_element_type=F32)


def dot_tn(a, b):
    return lax.dot_general(a, b, (((0,), (0,)), ((), ())), preferred_element_type=F32)


def dot_nn(a, b):
    return lax.dot_general(a, b, (((1,), (0,)), ((), ())), preferred_element_type=F32)


def spread(block, heads):
    lane = lax.broadcasted_iota(jnp.int32, block.shape, 1) // HDIM
    return jnp.concatenate(
        [jnp.where(lane == h, block, jnp.zeros_like(block)) for h in range(heads)], axis=0
    )


def pick(stacked, heads):
    rows = stacked.shape[0] // heads
    lane = lax.broadcasted_iota(jnp.int32, (rows, stacked.shape[1]), 1) // HDIM
    out = stacked[:rows]
    for h in range(1, heads):
        out = jnp.where(lane == h, stacked[h * rows : (h + 1) * rows], out)
    return out


def soft(scores, heads, valid=None):
    cols = scores.shape[1] // heads
    probs = []
    for h in range(heads):
        part = scores[:, h * cols : (h + 1) * cols] * SCALE
        if valid is not None:
            part = jnp.where(valid, part, -jnp.inf)
        raised = jnp.exp(part - jnp.max(part, axis=-1, keepdims=True))
        probs.append(raised / jnp.sum(raised, axis=-1, keepdims=True))
    return probs


def score_grad(probs, dprobs):
    cols = probs[0].shape[1]
    parts = []
    for h, prob in enumerate(probs):
        dpart = dprobs[:, h * cols : (h + 1) * cols]
        inner = jnp.sum(prob * dpart, axis=-1, keepdims=True)
        parts.append((prob * (dpart - inner) * SCALE).astype(BF))
    return jnp.concatenate(parts, axis=1)


def rounded(probs):
    return jnp.concatenate([p.astype(BF) for p in probs], axis=1)


PAIRS = 4


def spatial_fwd_kernel(q_ref, k_ref, v_ref, out_ref):
    for pair in range(PAIRS):
        cols = slice(pair * LANE, (pair + 1) * LANE)
        probs = soft(dot_nt(q_ref[:, cols], spread(k_ref[:, cols], 2)), 2)
        out_ref[:, cols] = dot_nn(rounded(probs), spread(v_ref[:, cols], 2)).astype(BF)


def spatial_fwd(q, k, v):
    spec = pl.BlockSpec((TOK, PAIRS * LANE), lambda i: (0, i))
    return pl.pallas_call(
        spatial_fwd_kernel,
        grid=(WIDTH // (PAIRS * LANE),),
        in_specs=[spec] * 3,
        out_specs=spec,
        out_shape=jax.ShapeDtypeStruct((TOK, WIDTH), BF),
        compiler_params=params(),
        name="spatial_fwd",
        cost_estimate=cost(4),
    )(q, k, v)


def spatial_bwd_kernel(gi_ref, w_ref, q_ref, k_ref, v_ref, dq_ref, dk_ref, dv_ref):
    dmixed = dot_nn(gi_ref[...], w_ref[...]).astype(BF)
    for pair in range(PAIRS):
        cols = slice(pair * LANE, (pair + 1) * LANE)
        q, dout = q_ref[:, cols], dmixed[:, cols]
        keys, values = spread(k_ref[:, cols], 2), spread(v_ref[:, cols], 2)
        probs = soft(dot_nt(q, keys), 2)
        dscores = score_grad(probs, dot_nt(dout, values))
        dv_ref[:, cols] = pick(dot_tn(rounded(probs), dout), 2).astype(BF)
        dq_ref[:, cols] = dot_nn(dscores, keys).astype(BF)
        dk_ref[:, cols] = pick(dot_tn(dscores, q), 2).astype(BF)


def spatial_bwd(grad_input, whole_out, q, k, v):
    spec = pl.BlockSpec((TOK, PAIRS * LANE), lambda i: (0, i))
    return pl.pallas_call(
        spatial_bwd_kernel,
        grid=(WIDTH // (PAIRS * LANE),),
        in_specs=[
            pl.BlockSpec((TOK, WIDTH), lambda i: (0, 0)),
            pl.BlockSpec((WIDTH, PAIRS * LANE), lambda i: (0, i)),
        ]
        + [spec] * 3,
        out_specs=[spec] * 3,
        out_shape=[jax.ShapeDtypeStruct((TOK, WIDTH), BF)] * 3,
        compiler_params=params(),
        name="spatial_bwd",
        cost_estimate=cost(9),
    )(grad_input, whole_out, q, k, v)


OUT_BLOCK = 512


def out_norm_kernel(mixed_ref, w_ref, in_ref, gain_ref, hidden_ref, normed_ref):
    step = pl.program_id(0)
    block = in_ref[...].astype(F32) + dot_nt(mixed_ref[...], w_ref[...])
    start = pl.multiple_of(step * OUT_BLOCK, OUT_BLOCK)
    hidden_ref[:, pl.ds(start, OUT_BLOCK)] = block.astype(BF)

    @pl.when(step == pl.num_programs(0) - 1)
    def _():
        wide = hidden_ref[...].astype(F32)
        inverse = lax.rsqrt(jnp.mean(wide * wide, axis=-1, keepdims=True) + EPSILON)
        normed_ref[...] = (wide * inverse * gain_ref[...]).astype(BF)


def out_norm(mixed, whole_out, inputs, gain):
    whole = pl.BlockSpec((TOK, WIDTH), lambda i: (0, 0))
    return pl.pallas_call(
        out_norm_kernel,
        grid=(WIDTH // OUT_BLOCK,),
        in_specs=[
            whole,
            pl.BlockSpec((OUT_BLOCK, WIDTH), lambda i: (i, 0)),
            pl.BlockSpec((TOK, OUT_BLOCK), lambda i: (0, i)),
            pl.BlockSpec((1, WIDTH), lambda i: (0, 0)),
        ],
        out_specs=[whole, whole],
        out_shape=[jax.ShapeDtypeStruct((TOK, WIDTH), BF)] * 2,
        compiler_params=params(),
        name="out_norm",
        cost_estimate=cost(4),
    )(mixed, whole_out, inputs, gain)


PADDED = 256
THREE = 3 * PADDED


def widen_kernel(w_ref, out_ref):
    rows = w_ref.shape[0]
    block = w_ref[...]
    for j in range(3):
        for h in range(3):
            out_ref[:, j * PADDED + h * HDIM : j * PADDED + (h + 1) * HDIM] = block[
                :, (h * 3 + j) * HDIM : (h * 3 + j + 1) * HDIM
            ]
        out_ref[:, j * PADDED + GROUP : (j + 1) * PADDED] = jnp.zeros((rows, PADDED - GROUP), BF)


def widen(weights):
    rows = 768
    return pl.pallas_call(
        widen_kernel,
        grid=(WIDTH // rows,),
        in_specs=[pl.BlockSpec((rows, THREE), lambda i: (i, WIDTH // THREE))],
        out_specs=pl.BlockSpec((rows, THREE), lambda i: (i, 0)),
        out_shape=jax.ShapeDtypeStruct((WIDTH, THREE), BF),
        compiler_params=params(),
        name="widen",
        cost_estimate=cost(1.5),
    )(weights)


POS = 16
CHAINS = 4


def temporal_block(q, keys, values, dout, valid):
    keys, values = spread(keys, 3), spread(values, 3)
    probs = soft(dot_nt(q, keys), 3, valid)
    prob_round = rounded(probs)
    dscores = score_grad(probs, dot_nt(dout, values))
    return dot_nn(prob_round, values).astype(BF), (
        dot_nn(dscores, keys).astype(BF),
        pick(dot_tn(dscores, q), 3).astype(BF),
        pick(dot_tn(prob_round, dout), 3).astype(BF),
    )


def temporal_kernel(order_ref, *refs):
    proj, (grad_ref, out_ref, dproj_ref) = refs[:SEQ], refs[SEQ:]
    shape = (SEQ * POS, SEQ * POS)
    valid = (
        lax.broadcasted_iota(jnp.int32, shape, 0) % POS
        == lax.broadcasted_iota(jnp.int32, shape, 1) % POS
    )
    for chain in range(CHAINS):
        place = slice(chain * POS, (chain + 1) * POS)

        def rows(j):
            return jnp.concatenate(
                [p[place, j * PADDED : j * PADDED + GROUP] for p in proj], axis=0
            )

        dout = jnp.concatenate([grad_ref[order_ref[r], place] for r in range(SEQ)], axis=0)
        heads_out, grads = temporal_block(rows(0), rows(1), rows(2), dout, valid)
        for r in range(SEQ):
            here = slice(r * POS, (r + 1) * POS)
            out_ref[order_ref[r], place] = heads_out[here]
            for j in range(3):
                dproj_ref[r, place, j * PADDED : j * PADDED + GROUP] = grads[j][here]
                dproj_ref[r, place, j * PADDED + GROUP : (j + 1) * PADDED] = jnp.zeros(
                    (POS, PADDED - GROUP), BF
                )


def temporal(order, proj, grad_heads):
    rows = CHAINS * POS
    frame = pl.BlockSpec((rows, THREE), lambda i, o: (i, 0))
    heads = pl.BlockSpec((SEQ, rows, GROUP), lambda i, o: (0, i, 0))
    return pl.pallas_call(
        temporal_kernel,
        grid_spec=pltpu.PrefetchScalarGridSpec(
            num_scalar_prefetch=1,
            grid=(TOK // rows,),
            in_specs=[frame] * SEQ + [heads],
            out_specs=[heads, pl.BlockSpec((SEQ, rows, THREE), lambda i, o: (0, i, 0))],
        ),
        out_shape=[
            jax.ShapeDtypeStruct((SEQ, TOK, GROUP), BF),
            jax.ShapeDtypeStruct((SEQ, TOK, THREE), BF),
        ],
        compiler_params=params(),
        name="temporal",
        cost_estimate=cost(8),
    )(order, *proj, grad_heads)


SHARE_COLS = 512


def shares_kernel(dproj_ref, w_ref, *outs):
    left = dproj_ref[...].reshape(len(outs) * TOK, THREE)
    full = dot_nt(left, w_ref[...]).astype(BF)
    for r, out in enumerate(outs):
        out[...] = full[r * TOK : (r + 1) * TOK]


def shares_of(dproj, wide_proj, half):
    count = SEQ // 2
    return pl.pallas_call(
        shares_kernel,
        grid=(WIDTH // SHARE_COLS,),
        in_specs=[
            pl.BlockSpec((count, TOK, THREE), lambda i: (half, 0, 0)),
            pl.BlockSpec((SHARE_COLS, THREE), lambda i: (i, 0)),
        ],
        out_specs=[pl.BlockSpec((TOK, SHARE_COLS), lambda i: (0, i))] * count,
        out_shape=[jax.ShapeDtypeStruct((TOK, WIDTH), BF)] * count,
        compiler_params=params(),
        name="shares",
        cost_estimate=cost(2),
    )(dproj, wide_proj)


GRAD_ROWS = 512


def qkv_grad_kernel(factor, *refs):
    frames, dproj_ref, out_ref = refs[:-2], refs[-2], refs[-1]
    left = jnp.concatenate([f[...] for f in frames], axis=0)
    right = dproj_ref[...].reshape(SEQ * TOK, THREE)
    full = (dot_tn(left, right) * factor).astype(BF)
    for j in range(3):
        for h in range(3):
            out_ref[:, (h * 3 + j) * HDIM : (h * 3 + j + 1) * HDIM] = full[
                :, j * PADDED + h * HDIM : j * PADDED + (h + 1) * HDIM
            ]


def qkv_product(frames, dproj, factor):
    return pl.pallas_call(
        functools.partial(qkv_grad_kernel, factor),
        grid=(WIDTH // GRAD_ROWS,),
        in_specs=[pl.BlockSpec((f.shape[0], GRAD_ROWS), lambda i: (0, i)) for f in frames]
        + [pl.BlockSpec((SEQ, TOK, THREE), lambda i: (0, 0, 0))],
        out_specs=pl.BlockSpec((GRAD_ROWS, 3 * GROUP), lambda i: (i, 0)),
        out_shape=jax.ShapeDtypeStruct((WIDTH, 3 * GROUP), BF),
        compiler_params=params(),
        name="qkv_product",
        cost_estimate=cost(5),
    )(*frames, dproj)


SHARE = 12
SLOT = 16
FOUR = 4
EXTRA = 16
GROUPED = DP * SLOT


def mover():
    shape = (FOUR * SHARE * SEQ, FOUR * SLOT * SEQ)
    source = lax.broadcasted_iota(jnp.int32, shape, 0)
    target = lax.broadcasted_iota(jnp.int32, shape, 1)
    group = target // (FOUR * SLOT)
    block = (target // SLOT) % FOUR
    turn = target % SLOT
    wanted = block * (SHARE * SEQ) + group * SHARE + turn
    return jnp.where((source == wanted) & (turn < SHARE), 1.0, 0.0).astype(BF)


def two_parts(row):
    high = row.astype(BF)
    return high, (row - high.astype(F32)).astype(BF)


def grad_input_kernel(factor, sum_a, sum_b, sum_c, sum_d, hidden_ref, resid_ref, gain_ref,
                      heads_ref, out_ref, groups_ref):
    def wide(ref):
        return ref[...].astype(F32)

    dnormed = (wide(sum_a) + wide(sum_b) + wide(sum_c) + wide(sum_d)).astype(BF).astype(F32)
    hidden = wide(hidden_ref)
    inverse = lax.rsqrt(jnp.mean(hidden * hidden, axis=-1, keepdims=True) + EPSILON)
    unit = hidden * inverse
    gain_high, gain_low = two_parts(jnp.sum(dnormed * unit, axis=0, keepdims=True) * factor)
    scaled = dnormed * gain_ref[...]
    through = inverse * (scaled - unit * jnp.mean(scaled * unit, axis=-1, keepdims=True))
    grad = (wide(resid_ref) + through).astype(BF)
    out_ref[...] = grad
    row = lax.broadcasted_iota(jnp.int32, (EXTRA, WIDTH), 0)
    extra = jnp.where(row == 0, gain_high.astype(F32), jnp.where(row == 1, gain_low.astype(F32), 0.0))
    both = jnp.concatenate([grad, extra.astype(BF)], axis=0)
    move = mover()
    rows, cols = FOUR * SHARE * SEQ, FOUR * SLOT
    for four in range(DP // FOUR):
        moved = dot_nn(both[:, four * rows : (four + 1) * rows], move).astype(BF)
        for j in range(SEQ):
            groups_ref[j, :, four * cols : (four + 1) * cols] = moved[:, j * cols : (j + 1) * cols]
    groups_ref[:, :TOK, GROUPED:] = heads_ref[...]
    groups_ref[:, TOK:, GROUPED:] = jnp.zeros((SEQ, EXTRA, GROUP), BF)


def grad_input_call(sums, hidden, resid, gain, heads_out, factor):
    return pl.pallas_call(
        functools.partial(grad_input_kernel, factor),
        out_shape=[
            jax.ShapeDtypeStruct((TOK, WIDTH), BF),
            jax.ShapeDtypeStruct((SEQ, TOK + EXTRA, GROUPED + GROUP), BF),
        ],
        compiler_params=params(),
        name="grad_input",
        cost_estimate=cost(2),
    )(*sums, hidden, resid, gain, heads_out)


def out_product_kernel(factor, order_ref, groups_ref, mixed_ref, mine_ref, other_ref):
    left = jnp.concatenate([groups_ref[order_ref[r], :TOK] for r in range(SEQ)], axis=0)
    product = dot_tn(left, mixed_ref[...]) * factor
    extras = sum(groups_ref[r, TOK:].astype(F32) for r in range(SEQ))
    high, low = two_parts(extras[0:1] + extras[1:2])
    turn = lax.broadcasted_iota(jnp.int32, (GROUPED, GROUPED), 0) % SLOT
    first = pl.program_id(0) == 0
    begin = product[:, :GROUPED]
    for place, part in ((SHARE, high), (SHARE + 1, low)):
        begin = jnp.where((turn == place) & first, part.astype(F32), begin)
    product = jnp.concatenate([begin, product[:, GROUPED:]], axis=1).astype(BF)
    first_core = order_ref[SEQ] == 0
    for d in range(DP // 2):
        even = product[2 * d * SLOT : (2 * d + 1) * SLOT]
        odd = product[(2 * d + 1) * SLOT : (2 * d + 2) * SLOT]
        mine_ref[d] = jnp.where(first_core, even, odd)
        other_ref[d] = jnp.where(first_core, odd, even)


def out_product(order, groups, mixed_all, factor):
    cols = 512
    spec = pl.BlockSpec((DP // 2, SLOT, cols), lambda i, o: (0, 0, i))
    return pl.pallas_call(
        functools.partial(out_product_kernel, factor),
        grid_spec=pltpu.PrefetchScalarGridSpec(
            num_scalar_prefetch=1,
            grid=(WIDTH // cols,),
            in_specs=[
                pl.BlockSpec((SEQ, TOK + EXTRA, GROUPED), lambda i, o: (0, 0, 0)),
                pl.BlockSpec((SEQ * TOK, cols), lambda i, o: (0, i)),
            ],
            out_specs=[spec, spec],
        ),
        out_shape=[jax.ShapeDtypeStruct((DP // 2, SLOT, WIDTH), BF)] * 2,
        compiler_params=params(),
        name="out_product",
        cost_estimate=cost(3),
    )(order, groups, mixed_all)


def fold_kernel(in_ref, out_ref):
    total = in_ref[0].astype(F32)
    for d in range(1, DP // 2):
        total = total + in_ref[d].astype(F32)
    high, low = two_parts(total[SHARE : SHARE + 1] + total[SHARE + 1 : SHARE + 2])
    turn = lax.broadcasted_iota(jnp.int32, total.shape, 0)
    total = jnp.where(turn == SHARE, high.astype(F32), total)
    total = jnp.where(turn == SHARE + 1, low.astype(F32), total).astype(BF)
    for j in range(SEQ):
        out_ref[j] = total


def fold(pieces):
    return pl.pallas_call(
        fold_kernel,
        out_shape=jax.ShapeDtypeStruct((SEQ, SLOT, WIDTH), BF),
        compiler_params=params(),
        name="fold",
        cost_estimate=cost(1.5),
    )(pieces)


def finish_kernel(in_ref, qkv_ref, out_ref, gain_ref, qkv_out_ref):
    qkv_out_ref[...] = qkv_ref[...].astype(F32)
    out_ref[...] = jnp.concatenate(
        [in_ref[j].astype(F32)[:SHARE] for j in range(SEQ)], axis=0
    )
    move = mover()
    rows, cols = FOUR * SHARE * SEQ, FOUR * SLOT
    for four in range(DP // FOUR):
        left = jnp.concatenate(
            [in_ref[j, :, four * cols : (four + 1) * cols] for j in range(SEQ)], axis=1
        )
        back = dot_nt(left, move)
        gain_ref[pl.ds(four * rows, rows)] = back[SHARE] + back[SHARE + 1]


def finish(gathered, qkv_rows):
    return pl.pallas_call(
        finish_kernel,
        out_shape=[
            jax.ShapeDtypeStruct((SEQ * SHARE, WIDTH), F32),
            jax.ShapeDtypeStruct((WIDTH,), F32),
            jax.ShapeDtypeStruct(qkv_rows.shape, F32),
        ],
        compiler_params=params(),
        name="finish",
        cost_estimate=cost(2),
    )(gathered, qkv_rows)


def along_x(array, shift):
    pairs = [(i, ((i // 2 + shift) % XS) * 2 + i % 2) for i in range(SEQ)]
    return lax.ppermute(array, "seq", pairs)


def across_y(array):
    return lax.ppermute(array, "seq", [(i, i ^ 1) for i in range(SEQ)])


HALF = TOK // 2


def gather_frames(own):
    behind, ahead, partner = along_x(own, 1), along_x(own, -1), across_y(own)
    far_top, far_low = along_x(behind[:HALF], 1), along_x(ahead[HALF:], -1)
    partner_behind, partner_ahead = along_x(partner, 1), along_x(partner, -1)
    return (
        own, behind, ahead, far_top, far_low,
        partner, partner_behind, partner_ahead, across_y(far_top), across_y(far_low),
    )


def gather_along_x(own):
    behind, ahead, partner = along_x(own, 1), along_x(own, -1), across_y(own)
    far_top, far_low = along_x(behind[:HALF], 1), along_x(ahead[HALF:], -1)
    partner_behind, partner_ahead = along_x(partner, 1), along_x(partner, -1)
    partner_top, partner_low = along_x(partner_behind[:HALF], 1), along_x(partner_ahead[HALF:], -1)
    return (
        own, behind, ahead, far_top, far_low,
        partner, partner_behind, partner_ahead, partner_top, partner_low,
    )


def whole_frames(parts):
    own, behind, ahead, top, low, partner, pbehind, pahead, ptop, plow = parts
    return (
        own, behind, ahead, jnp.concatenate([top, low], axis=0),
        partner, pbehind, pahead, jnp.concatenate([ptop, plow], axis=0),
    )


def scatter_frames(shares):
    own, behind, ahead, far, partner, pbehind, pahead, far_share = shares
    far = far + far_share
    partner = partner + along_x(pbehind, -1) + along_x(pahead, 1)
    top, low = along_x(far[:HALF], -1), along_x(far[HALF:], 1)
    behind = jnp.concatenate([behind[:HALF] + top, behind[HALF:]], axis=0)
    ahead = jnp.concatenate([ahead[:HALF], ahead[HALF:] + low], axis=0)
    return own, across_y(partner), along_x(behind, -1), along_x(ahead, 1)


def chip_exchange(blocks):
    groups = [[2 * i + c for i in range(DP // 2)] for c in range(2)]
    return lax.all_to_all(blocks, "dp", 0, 0, axis_index_groups=groups, tiled=True)


def body(
    inputs, spatial_q, spatial_k, spatial_v, out_weight, norm_gain, qkv_weight, grad_out, grad_resid
):
    block_shape = inputs.shape
    factor = (TOK * DP * SEQ) ** (-0.5)
    flat_in, q, k, v, dout, resid = (
        a.reshape(TOK, WIDTH)
        for a in (inputs, spatial_q, spatial_k, spatial_v, grad_out, grad_resid)
    )
    gain = norm_gain.reshape(1, WIDTH)
    me = lax.axis_index("seq")
    place_x, place_y = me // 2, me % 2
    order = jnp.stack(
        [((place_x + s) % XS) * 2 + y for y in (place_y, 1 - place_y) for s in (0, 3, 1, 2)]
        + [lax.axis_index("dp") % 2]
    ).astype(jnp.int32)

    filler = jnp.zeros((out_weight.shape[0], THREE - 3 * GROUP), BF)
    weights = lax.all_gather(
        jnp.concatenate([out_weight, qkv_weight, filler], axis=1), "dp", axis=0, tiled=True
    )
    mixed = spatial_fwd(q, k, v)
    grad_heads = lax.all_to_all(
        dout.reshape(TOK, SEQ, GROUP).transpose(1, 0, 2), "seq", 0, 0, tiled=True
    )
    mixed_parts = gather_along_x(mixed)
    mixed_all = jnp.concatenate(mixed_parts, axis=0)
    weights, grad_heads, mixed_all = lax.optimization_barrier((weights, grad_heads, mixed_all))
    hidden, normed = out_norm(mixed, weights, flat_in, gain)
    normed_parts = gather_frames(normed)
    proj_weights, *first = lax.optimization_barrier((weights, *normed_parts[:3], normed_parts[5]))
    frames = (*first[:3], *normed_parts[3:5], first[3], *normed_parts[6:])
    wide_proj = widen(proj_weights)
    proj = [dot_nn(f, wide_proj).astype(BF) for f in whole_frames(frames)]
    heads_out, dproj = temporal(order, proj, grad_heads)
    partner_shares = shares_of(dproj, wide_proj, 1)
    *partner_shares, dproj = lax.optimization_barrier((*partner_shares, dproj))
    far_share, dproj_later = lax.optimization_barrier((across_y(partner_shares[3]), dproj))
    qkv_share = qkv_product(normed_parts, dproj_later, factor)
    qkv_grad = lax.psum_scatter(qkv_share, "dp", scatter_dimension=0, tiled=True)
    sums = scatter_frames((*shares_of(dproj, wide_proj, 0), *partner_shares[:3], far_share))

    grad_input, groups = grad_input_call(sums, hidden, resid, gain, heads_out, factor)
    groups = lax.all_to_all(groups, "seq", 0, 0, tiled=True)
    grads = spatial_bwd(grad_input, weights, q, k, v)
    groups, *grads = lax.optimization_barrier((groups, *grads))
    mine, other = out_product(order, groups, mixed_all, factor)
    summed = mine + lax.ppermute(other, "dp", [(i, i ^ 1) for i in range(DP)])
    received = chip_exchange(summed)
    temporal_out = groups[:, :TOK, GROUPED:].transpose(1, 0, 2).reshape(TOK, WIDTH)
    gathered = lax.all_to_all(fold(received), "seq", 0, 0, tiled=True)
    out_grad, gain_grad, qkv_grad = finish(gathered, qkv_grad)
    return tuple(a.reshape(block_shape) for a in (hidden, temporal_out, grad_input, *grads)) + (
        qkv_grad,
        out_grad,
        gain_grad,
    )


def solution(mesh):
    tokens = P("dp", "seq", None, None, None)
    return jax.shard_map(
        body,
        mesh=mesh,
        in_specs=(
            tokens, tokens, tokens, tokens, P("dp", None), P(), P("dp", "seq"), tokens, tokens,
        ),
        out_specs=(
            tokens, tokens, tokens, tokens, tokens, tokens, P("dp", "seq"), P("dp", None), P(),
        ),
        check_vma=False,
    )
```

```python
import functools

import jax
import jax.numpy as jnp
from jax import lax
from jax.experimental import pallas as pl
from jax.experimental.pallas import tpu as pltpu
from jax.sharding import PartitionSpec as P

HEADS = 24
HDIM = 64
EPSILON = 1e-06
XS = 4
SEQ = 8
DP = 16
TOK = 128
WIDTH = HEADS * HDIM
GROUP = WIDTH // SEQ
LANE = 128
BF = jnp.bfloat16
F32 = jnp.float32
SCALE = HDIM**-0.5
VMEM_LIMIT = 20 * 1024 * 1024
HBM_RATE = 3_000_000


def params(limit=VMEM_LIMIT):
    return pltpu.CompilerParams(vmem_limit_bytes=limit)


def cost(micros):
    return pl.CostEstimate(flops=0, bytes_accessed=int(micros * HBM_RATE), transcendentals=0)


def dot_nt(a, b):
    return lax.dot_general(a, b, (((1,), (1,)), ((), ())), preferred_element_type=F32)


def dot_tn(a, b):
    return lax.dot_general(a, b, (((0,), (0,)), ((), ())), preferred_element_type=F32)


def dot_nn(a, b):
    return lax.dot_general(a, b, (((1,), (0,)), ((), ())), preferred_element_type=F32)


def spread(block, heads):
    lane = lax.broadcasted_iota(jnp.int32, block.shape, 1) // HDIM
    return jnp.concatenate(
        [jnp.where(lane == h, block, jnp.zeros_like(block)) for h in range(heads)], axis=0
    )


def pick(stacked, heads):
    rows = stacked.shape[0] // heads
    lane = lax.broadcasted_iota(jnp.int32, (rows, stacked.shape[1]), 1) // HDIM
    out = stacked[:rows]
    for h in range(1, heads):
        out = jnp.where(lane == h, stacked[h * rows : (h + 1) * rows], out)
    return out


def soft(scores, heads, valid=None):
    cols = scores.shape[1] // heads
    probs = []
    for h in range(heads):
        part = scores[:, h * cols : (h + 1) * cols] * SCALE
        if valid is not None:
            part = jnp.where(valid, part, -jnp.inf)
        raised = jnp.exp(part - jnp.max(part, axis=-1, keepdims=True))
        probs.append(raised / jnp.sum(raised, axis=-1, keepdims=True))
    return probs


def score_grad(probs, dprobs):
    cols = probs[0].shape[1]
    parts = []
    for h, prob in enumerate(probs):
        dpart = dprobs[:, h * cols : (h + 1) * cols]
        inner = jnp.sum(prob * dpart, axis=-1, keepdims=True)
        parts.append((prob * (dpart - inner) * SCALE).astype(BF))
    return jnp.concatenate(parts, axis=1)


def rounded(probs):
    return jnp.concatenate([p.astype(BF) for p in probs], axis=1)


PAIRS = 4


def spatial_fwd_kernel(q_ref, k_ref, v_ref, out_ref):
    for pair in range(PAIRS):
        cols = slice(pair * LANE, (pair + 1) * LANE)
        probs = soft(dot_nt(q_ref[:, cols], spread(k_ref[:, cols], 2)), 2)
        out_ref[:, cols] = dot_nn(rounded(probs), spread(v_ref[:, cols], 2)).astype(BF)


def spatial_fwd(q, k, v):
    spec = pl.BlockSpec((TOK, PAIRS * LANE), lambda i: (0, i))
    return pl.pallas_call(
        spatial_fwd_kernel,
        grid=(WIDTH // (PAIRS * LANE),),
        in_specs=[spec] * 3,
        out_specs=spec,
        out_shape=jax.ShapeDtypeStruct((TOK, WIDTH), BF),
        compiler_params=params(),
        name="spatial_fwd",
        cost_estimate=cost(4),
    )(q, k, v)


def spatial_bwd_kernel(gi_ref, w_ref, q_ref, k_ref, v_ref, dq_ref, dk_ref, dv_ref):
    dmixed = dot_nn(gi_ref[...], w_ref[...]).astype(BF)
    for pair in range(PAIRS):
        cols = slice(pair * LANE, (pair + 1) * LANE)
        q, dout = q_ref[:, cols], dmixed[:, cols]
        keys, values = spread(k_ref[:, cols], 2), spread(v_ref[:, cols], 2)
        probs = soft(dot_nt(q, keys), 2)
        dscores = score_grad(probs, dot_nt(dout, values))
        dv_ref[:, cols] = pick(dot_tn(rounded(probs), dout), 2).astype(BF)
        dq_ref[:, cols] = dot_nn(dscores, keys).astype(BF)
        dk_ref[:, cols] = pick(dot_tn(dscores, q), 2).astype(BF)


def spatial_bwd(grad_input, whole_out, q, k, v):
    spec = pl.BlockSpec((TOK, PAIRS * LANE), lambda i: (0, i))
    return pl.pallas_call(
        spatial_bwd_kernel,
        grid=(WIDTH // (PAIRS * LANE),),
        in_specs=[
            pl.BlockSpec((TOK, WIDTH), lambda i: (0, 0)),
            pl.BlockSpec((WIDTH, PAIRS * LANE), lambda i: (0, i)),
        ]
        + [spec] * 3,
        out_specs=[spec] * 3,
        out_shape=[jax.ShapeDtypeStruct((TOK, WIDTH), BF)] * 3,
        compiler_params=params(),
        name="spatial_bwd",
        cost_estimate=cost(9),
    )(grad_input, whole_out, q, k, v)


OUT_BLOCK = 512


PADDED = 256
THREE = 3 * PADDED


def widen(block, out_ref):
    for j in range(3):
        for h in range(3):
            out_ref[:, j * PADDED + h * HDIM : j * PADDED + (h + 1) * HDIM] = block[
                :, (h * 3 + j) * HDIM : (h * 3 + j + 1) * HDIM
            ]
        out_ref[:, j * PADDED + GROUP : (j + 1) * PADDED] = jnp.zeros(
            (block.shape[0], PADDED - GROUP), BF
        )


def out_norm_kernel(mixed_ref, w_ref, in_ref, gain_ref, hidden_ref, normed_ref, wide_ref):
    step = pl.program_id(0)
    block = in_ref[...].astype(F32) + dot_nt(mixed_ref[...], w_ref[:, :WIDTH])
    start = pl.multiple_of(step * OUT_BLOCK, OUT_BLOCK)
    hidden_ref[:, pl.ds(start, OUT_BLOCK)] = block.astype(BF)
    widen(w_ref[:, WIDTH:], wide_ref)

    @pl.when(step == pl.num_programs(0) - 1)
    def _():
        wide = hidden_ref[...].astype(F32)
        inverse = lax.rsqrt(jnp.mean(wide * wide, axis=-1, keepdims=True) + EPSILON)
        normed_ref[...] = (wide * inverse * gain_ref[...]).astype(BF)


def out_norm(mixed, weights, inputs, gain):
    whole = pl.BlockSpec((TOK, WIDTH), lambda i: (0, 0))
    return pl.pallas_call(
        out_norm_kernel,
        grid=(WIDTH // OUT_BLOCK,),
        in_specs=[
            whole,
            pl.BlockSpec((OUT_BLOCK, weights.shape[1]), lambda i: (i, 0)),
            pl.BlockSpec((TOK, OUT_BLOCK), lambda i: (0, i)),
            pl.BlockSpec((1, WIDTH), lambda i: (0, 0)),
        ],
        out_specs=[whole, whole, pl.BlockSpec((OUT_BLOCK, THREE), lambda i: (i, 0))],
        out_shape=[jax.ShapeDtypeStruct((TOK, WIDTH), BF)] * 2
        + [jax.ShapeDtypeStruct((WIDTH, THREE), BF)],
        compiler_params=params(58 * 1024 * 1024),
        name="out_norm",
        cost_estimate=cost(5),
    )(mixed, weights, inputs, gain)


POS = 16
CHAINS = 4


def temporal_block(q, keys, values, dout, valid):
    keys, values = spread(keys, 3), spread(values, 3)
    probs = soft(dot_nt(q, keys), 3, valid)
    prob_round = rounded(probs)
    dscores = score_grad(probs, dot_nt(dout, values))
    return dot_nn(prob_round, values).astype(BF), (
        dot_nn(dscores, keys).astype(BF),
        pick(dot_tn(dscores, q), 3).astype(BF),
        pick(dot_tn(prob_round, dout), 3).astype(BF),
    )


def temporal_kernel(order_ref, *refs):
    proj, (grad_ref, out_ref, dproj_ref) = refs[:SEQ], refs[SEQ:]
    shape = (SEQ * POS, SEQ * POS)
    valid = (
        lax.broadcasted_iota(jnp.int32, shape, 0) % POS
        == lax.broadcasted_iota(jnp.int32, shape, 1) % POS
    )
    for chain in range(CHAINS):
        place = slice(chain * POS, (chain + 1) * POS)

        def rows(j):
            return jnp.concatenate(
                [p[place, j * PADDED : j * PADDED + GROUP] for p in proj], axis=0
            )

        dout = jnp.concatenate([grad_ref[order_ref[r], place] for r in range(SEQ)], axis=0)
        heads_out, grads = temporal_block(rows(0), rows(1), rows(2), dout, valid)
        for r in range(SEQ):
            here = slice(r * POS, (r + 1) * POS)
            out_ref[order_ref[r], place] = heads_out[here]
            for j in range(3):
                dproj_ref[r, place, j * PADDED : j * PADDED + GROUP] = grads[j][here]
                dproj_ref[r, place, j * PADDED + GROUP : (j + 1) * PADDED] = jnp.zeros(
                    (POS, PADDED - GROUP), BF
                )


def temporal(order, proj, grad_heads):
    rows = CHAINS * POS
    frame = pl.BlockSpec((rows, THREE), lambda i, o: (i, 0))
    heads = pl.BlockSpec((SEQ, rows, GROUP), lambda i, o: (0, i, 0))
    return pl.pallas_call(
        temporal_kernel,
        grid_spec=pltpu.PrefetchScalarGridSpec(
            num_scalar_prefetch=1,
            grid=(TOK // rows,),
            in_specs=[frame] * SEQ + [heads],
            out_specs=[heads, pl.BlockSpec((SEQ, rows, THREE), lambda i, o: (0, i, 0))],
        ),
        out_shape=[
            jax.ShapeDtypeStruct((SEQ, TOK, GROUP), BF),
            jax.ShapeDtypeStruct((SEQ, TOK, THREE), BF),
        ],
        compiler_params=params(),
        name="temporal",
        cost_estimate=cost(8),
    )(order, *proj, grad_heads)


SHARE_COLS = 512


def shares_kernel(dproj_ref, w_ref, *outs):
    left = dproj_ref[...].reshape(len(outs) * TOK, THREE)
    full = dot_nt(left, w_ref[...]).astype(BF)
    for r, out in enumerate(outs):
        out[...] = full[r * TOK : (r + 1) * TOK]


def shares_of(dproj, wide_proj, half):
    count = SEQ // 2
    return pl.pallas_call(
        shares_kernel,
        grid=(WIDTH // SHARE_COLS,),
        in_specs=[
            pl.BlockSpec((count, TOK, THREE), lambda i: (half, 0, 0)),
            pl.BlockSpec((SHARE_COLS, THREE), lambda i: (i, 0)),
        ],
        out_specs=[pl.BlockSpec((TOK, SHARE_COLS), lambda i: (0, i))] * count,
        out_shape=[jax.ShapeDtypeStruct((TOK, WIDTH), BF)] * count,
        compiler_params=params(),
        name="shares",
        cost_estimate=cost(2),
    )(dproj, wide_proj)


GRAD_ROWS = 512


def qkv_grad_kernel(factor, *refs):
    frames, dproj_ref, out_ref = refs[:-2], refs[-2], refs[-1]
    left = jnp.concatenate([f[...] for f in frames], axis=0)
    right = dproj_ref[...].reshape(SEQ * TOK, THREE)
    full = (dot_tn(left, right) * factor).astype(BF)
    for j in range(3):
        for h in range(3):
            out_ref[:, (h * 3 + j) * HDIM : (h * 3 + j + 1) * HDIM] = full[
                :, j * PADDED + h * HDIM : j * PADDED + (h + 1) * HDIM
            ]


def qkv_product(frames, dproj, factor):
    return pl.pallas_call(
        functools.partial(qkv_grad_kernel, factor),
        grid=(WIDTH // GRAD_ROWS,),
        in_specs=[pl.BlockSpec((f.shape[0], GRAD_ROWS), lambda i: (0, i)) for f in frames]
        + [pl.BlockSpec((SEQ, TOK, THREE), lambda i: (0, 0, 0))],
        out_specs=pl.BlockSpec((GRAD_ROWS, 3 * GROUP), lambda i: (i, 0)),
        out_shape=jax.ShapeDtypeStruct((WIDTH, 3 * GROUP), BF),
        compiler_params=params(),
        name="qkv_product",
        cost_estimate=cost(5),
    )(*frames, dproj)


SHARE = 12
SLOT = 16
FOUR = 4
EXTRA = 16
GROUPED = DP * SLOT


def mover():
    shape = (FOUR * SHARE * SEQ, FOUR * SLOT * SEQ)
    source = lax.broadcasted_iota(jnp.int32, shape, 0)
    target = lax.broadcasted_iota(jnp.int32, shape, 1)
    group = target // (FOUR * SLOT)
    block = (target // SLOT) % FOUR
    turn = target % SLOT
    wanted = block * (SHARE * SEQ) + group * SHARE + turn
    return jnp.where((source == wanted) & (turn < SHARE), 1.0, 0.0).astype(BF)


def two_parts(row):
    high = row.astype(BF)
    return high, (row - high.astype(F32)).astype(BF)


def grad_input_kernel(factor, sum_a, sum_b, sum_c, sum_d, hidden_ref, resid_ref, gain_ref,
                      heads_ref, out_ref, groups_ref):
    def wide(ref):
        return ref[...].astype(F32)

    dnormed = (wide(sum_a) + wide(sum_b) + wide(sum_c) + wide(sum_d)).astype(BF).astype(F32)
    hidden = wide(hidden_ref)
    inverse = lax.rsqrt(jnp.mean(hidden * hidden, axis=-1, keepdims=True) + EPSILON)
    unit = hidden * inverse
    gain_high, gain_low = two_parts(jnp.sum(dnormed * unit, axis=0, keepdims=True) * factor)
    scaled = dnormed * gain_ref[...]
    through = inverse * (scaled - unit * jnp.mean(scaled * unit, axis=-1, keepdims=True))
    grad = (wide(resid_ref) + through).astype(BF)
    out_ref[...] = grad
    row = lax.broadcasted_iota(jnp.int32, (EXTRA, WIDTH), 0)
    extra = jnp.where(row == 0, gain_high.astype(F32), jnp.where(row == 1, gain_low.astype(F32), 0.0))
    both = jnp.concatenate([grad, extra.astype(BF)], axis=0)
    move = mover()
    rows, cols = FOUR * SHARE * SEQ, FOUR * SLOT
    for four in range(DP // FOUR):
        moved = dot_nn(both[:, four * rows : (four + 1) * rows], move).astype(BF)
        for j in range(SEQ):
            groups_ref[j, :, four * cols : (four + 1) * cols] = moved[:, j * cols : (j + 1) * cols]
    groups_ref[:, :TOK, GROUPED:] = heads_ref[...]
    groups_ref[:, TOK:, GROUPED:] = jnp.zeros((SEQ, EXTRA, GROUP), BF)


def grad_input_call(sums, hidden, resid, gain, heads_out, factor):
    return pl.pallas_call(
        functools.partial(grad_input_kernel, factor),
        out_shape=[
            jax.ShapeDtypeStruct((TOK, WIDTH), BF),
            jax.ShapeDtypeStruct((SEQ, TOK + EXTRA, GROUPED + GROUP), BF),
        ],
        compiler_params=params(),
        name="grad_input",
        cost_estimate=cost(2),
    )(*sums, hidden, resid, gain, heads_out)


def out_product_kernel(factor, order_ref, groups_ref, mixed_ref, mine_ref, other_ref):
    left = jnp.concatenate([groups_ref[order_ref[r], :TOK] for r in range(SEQ)], axis=0)
    product = dot_tn(left, mixed_ref[...]) * factor
    extras = sum(groups_ref[r, TOK:].astype(F32) for r in range(SEQ))
    high, low = two_parts(extras[0:1] + extras[1:2])
    turn = lax.broadcasted_iota(jnp.int32, (GROUPED, GROUPED), 0) % SLOT
    first = pl.program_id(0) == 0
    begin = product[:, :GROUPED]
    for place, part in ((SHARE, high), (SHARE + 1, low)):
        begin = jnp.where((turn == place) & first, part.astype(F32), begin)
    product = jnp.concatenate([begin, product[:, GROUPED:]], axis=1).astype(BF)
    first_core = order_ref[SEQ] == 0
    for d in range(DP // 2):
        even = product[2 * d * SLOT : (2 * d + 1) * SLOT]
        odd = product[(2 * d + 1) * SLOT : (2 * d + 2) * SLOT]
        mine_ref[d] = jnp.where(first_core, even, odd)
        other_ref[d] = jnp.where(first_core, odd, even)


def out_product(order, groups, mixed_all, factor):
    cols = 512
    spec = pl.BlockSpec((DP // 2, SLOT, cols), lambda i, o: (0, 0, i))
    return pl.pallas_call(
        functools.partial(out_product_kernel, factor),
        grid_spec=pltpu.PrefetchScalarGridSpec(
            num_scalar_prefetch=1,
            grid=(WIDTH // cols,),
            in_specs=[
                pl.BlockSpec((SEQ, TOK + EXTRA, GROUPED), lambda i, o: (0, 0, 0)),
                pl.BlockSpec((SEQ * TOK, cols), lambda i, o: (0, i)),
            ],
            out_specs=[spec, spec],
        ),
        out_shape=[jax.ShapeDtypeStruct((DP // 2, SLOT, WIDTH), BF)] * 2,
        compiler_params=params(),
        name="out_product",
        cost_estimate=cost(3),
    )(order, groups, mixed_all)


def fold_kernel(in_ref, out_ref):
    total = in_ref[0].astype(F32)
    for d in range(1, DP // 2):
        total = total + in_ref[d].astype(F32)
    high, low = two_parts(total[SHARE : SHARE + 1] + total[SHARE + 1 : SHARE + 2])
    turn = lax.broadcasted_iota(jnp.int32, total.shape, 0)
    total = jnp.where(turn == SHARE, high.astype(F32), total)
    total = jnp.where(turn == SHARE + 1, low.astype(F32), total).astype(BF)
    for j in range(SEQ):
        out_ref[j] = total


def fold(pieces):
    return pl.pallas_call(
        fold_kernel,
        out_shape=jax.ShapeDtypeStruct((SEQ, SLOT, WIDTH), BF),
        compiler_params=params(),
        name="fold",
        cost_estimate=cost(1.5),
    )(pieces)


def finish_kernel(in_ref, qkv_ref, out_ref, gain_ref, qkv_out_ref):
    qkv_out_ref[...] = qkv_ref[...].astype(F32)
    out_ref[...] = jnp.concatenate(
        [in_ref[j].astype(F32)[:SHARE] for j in range(SEQ)], axis=0
    )
    move = mover()
    rows, cols = FOUR * SHARE * SEQ, FOUR * SLOT
    for four in range(DP // FOUR):
        left = jnp.concatenate(
            [in_ref[j, :, four * cols : (four + 1) * cols] for j in range(SEQ)], axis=1
        )
        back = dot_nt(left, move)
        gain_ref[pl.ds(four * rows, rows)] = back[SHARE] + back[SHARE + 1]


def finish(gathered, qkv_rows):
    return pl.pallas_call(
        finish_kernel,
        out_shape=[
            jax.ShapeDtypeStruct((SEQ * SHARE, WIDTH), F32),
            jax.ShapeDtypeStruct((WIDTH,), F32),
            jax.ShapeDtypeStruct(qkv_rows.shape, F32),
        ],
        compiler_params=params(),
        name="finish",
        cost_estimate=cost(2),
    )(gathered, qkv_rows)


def along_x(array, shift):
    pairs = [(i, ((i // 2 + shift) % XS) * 2 + i % 2) for i in range(SEQ)]
    return lax.ppermute(array, "seq", pairs)


def across_y(array):
    return lax.ppermute(array, "seq", [(i, i ^ 1) for i in range(SEQ)])


HALF = TOK // 2


def gather_frames(own):
    behind, ahead, partner = along_x(own, 1), along_x(own, -1), across_y(own)
    far_top, far_low = along_x(behind[:HALF], 1), along_x(ahead[HALF:], -1)
    partner_behind, partner_ahead = along_x(partner, 1), along_x(partner, -1)
    return (
        own, behind, ahead, far_top, far_low,
        partner, partner_behind, partner_ahead, across_y(far_top), across_y(far_low),
    )


def gather_by_x(own):
    partner, behind, ahead, far = across_y(own), along_x(own, 1), along_x(own, -1), along_x(own, 2)
    return (
        own, behind, ahead, far,
        partner, along_x(partner, 1), along_x(partner, -1), along_x(partner, 2),
    )


def whole_frames(parts):
    own, behind, ahead, top, low, partner, pbehind, pahead, ptop, plow = parts
    return (
        own, behind, ahead, jnp.concatenate([top, low], axis=0),
        partner, pbehind, pahead, jnp.concatenate([ptop, plow], axis=0),
    )


def scatter_frames(own, behind, ahead, far, partner, from_pbehind, from_pahead):
    partner = partner + from_pbehind + from_pahead
    top, low = along_x(far[:HALF], -1), along_x(far[HALF:], 1)
    behind = jnp.concatenate([behind[:HALF] + top, behind[HALF:]], axis=0)
    ahead = jnp.concatenate([ahead[:HALF], ahead[HALF:] + low], axis=0)
    return own, across_y(partner), along_x(behind, -1), along_x(ahead, 1)


def chip_exchange(blocks):
    groups = [[2 * i + c for i in range(DP // 2)] for c in range(2)]
    return lax.all_to_all(blocks, "dp", 0, 0, axis_index_groups=groups, tiled=True)


def body(
    inputs, spatial_q, spatial_k, spatial_v, out_weight, norm_gain, qkv_weight, grad_out, grad_resid
):
    block_shape = inputs.shape
    factor = (TOK * DP * SEQ) ** (-0.5)
    flat_in, q, k, v, dout, resid = (
        a.reshape(TOK, WIDTH)
        for a in (inputs, spatial_q, spatial_k, spatial_v, grad_out, grad_resid)
    )
    gain = norm_gain.reshape(1, WIDTH)
    me = lax.axis_index("seq")
    place_x, place_y = me // 2, me % 2
    order = jnp.stack(
        [((place_x + s) % XS) * 2 + y for y in (place_y, 1 - place_y) for s in (0, 3, 1, 2)]
        + [lax.axis_index("dp") % 2]
    ).astype(jnp.int32)

    weights = lax.all_gather(
        jnp.concatenate([out_weight, qkv_weight], axis=1), "dp", axis=0, tiled=True
    )
    mixed = spatial_fwd(q, k, v)
    grad_heads = lax.all_to_all(
        dout.reshape(TOK, SEQ, GROUP).transpose(1, 0, 2), "seq", 0, 0, tiled=True
    )
    mixed_parts = gather_by_x(mixed)
    mixed_all = jnp.concatenate(mixed_parts, axis=0)
    weights, grad_heads, mixed_all = lax.optimization_barrier((weights, grad_heads, mixed_all))
    hidden, normed, wide_proj = out_norm(mixed, weights, flat_in, gain)
    normed_parts = gather_frames(normed)
    proj = [dot_nn(f, wide_proj).astype(BF) for f in whole_frames(normed_parts)]
    heads_out, dproj = temporal(order, proj, grad_heads)
    partner, pbehind, pahead, pfar = shares_of(dproj, wide_proj, 1)
    partner, pbehind, pahead, pfar, dproj = lax.optimization_barrier(
        (partner, pbehind, pahead, pfar, dproj)
    )
    qkv_share = qkv_product(normed_parts, dproj, factor)
    qkv_grad = lax.psum_scatter(qkv_share, "dp", scatter_dimension=0, tiled=True)
    pfar, pbehind, pahead = lax.optimization_barrier(
        (across_y(pfar), along_x(pbehind, -1), along_x(pahead, 1))
    )
    own, behind, ahead, far = shares_of(dproj, wide_proj, 0)
    sums = scatter_frames(own, behind, ahead, far + pfar, partner, pbehind, pahead)

    grad_input, groups = grad_input_call(sums, hidden, resid, gain, heads_out, factor)
    groups = lax.all_to_all(groups, "seq", 0, 0, tiled=True)
    grads = spatial_bwd(grad_input, weights, q, k, v)
    groups, *grads = lax.optimization_barrier((groups, *grads))
    mine, other = out_product(order, groups, mixed_all, factor)
    summed = mine + lax.ppermute(other, "dp", [(i, i ^ 1) for i in range(DP)])
    received = chip_exchange(summed)
    temporal_out = groups[:, :TOK, GROUPED:].transpose(1, 0, 2).reshape(TOK, WIDTH)
    gathered = lax.all_to_all(fold(received), "seq", 0, 0, tiled=True)
    out_grad, gain_grad, qkv_grad = finish(gathered, qkv_grad)
    return tuple(a.reshape(block_shape) for a in (hidden, temporal_out, grad_input, *grads)) + (
        qkv_grad,
        out_grad,
        gain_grad,
    )


def solution(mesh):
    tokens = P("dp", "seq", None, None, None)
    return jax.shard_map(
        body,
        mesh=mesh,
        in_specs=(
            tokens, tokens, tokens, tokens, P("dp", None), P(), P("dp", "seq"), tokens, tokens,
        ),
        out_specs=(
            tokens, tokens, tokens, tokens, tokens, tokens, P("dp", "seq"), P("dp", None), P(),
        ),
        check_vma=False,
    )
```

```python
import functools

import jax
import jax.numpy as jnp
from jax import lax
from jax.experimental import pallas as pl
from jax.experimental.pallas import tpu as pltpu
from jax.sharding import PartitionSpec as P

HEADS = 24
HDIM = 64
EPSILON = 1e-06
XS = 4
SEQ = 8
DP = 16
TOK = 128
WIDTH = HEADS * HDIM
GROUP = WIDTH // SEQ
LANE = 128
BF = jnp.bfloat16
F32 = jnp.float32
SCALE = HDIM**-0.5
VMEM_LIMIT = 20 * 1024 * 1024
VMEM_MOST = 58 * 1024 * 1024
HBM_RATE = 3_000_000


def params(limit=VMEM_LIMIT):
    return pltpu.CompilerParams(vmem_limit_bytes=limit)


def cost(micros):
    return pl.CostEstimate(flops=0, bytes_accessed=int(micros * HBM_RATE), transcendentals=0)


def dot_nt(a, b):
    return lax.dot_general(a, b, (((1,), (1,)), ((), ())), preferred_element_type=F32)


def dot_tn(a, b):
    return lax.dot_general(a, b, (((0,), (0,)), ((), ())), preferred_element_type=F32)


def dot_nn(a, b):
    return lax.dot_general(a, b, (((1,), (0,)), ((), ())), preferred_element_type=F32)


def spread(block, heads):
    lane = lax.broadcasted_iota(jnp.int32, block.shape, 1) // HDIM
    return jnp.concatenate(
        [jnp.where(lane == h, block, jnp.zeros_like(block)) for h in range(heads)], axis=0
    )


def pick(stacked, heads):
    rows = stacked.shape[0] // heads
    lane = lax.broadcasted_iota(jnp.int32, (rows, stacked.shape[1]), 1) // HDIM
    out = stacked[:rows]
    for h in range(1, heads):
        out = jnp.where(lane == h, stacked[h * rows : (h + 1) * rows], out)
    return out


def soft(scores, heads, valid=None):
    cols = scores.shape[1] // heads
    probs = []
    for h in range(heads):
        part = scores[:, h * cols : (h + 1) * cols] * SCALE
        if valid is not None:
            part = jnp.where(valid, part, -jnp.inf)
        raised = jnp.exp(part - jnp.max(part, axis=-1, keepdims=True))
        probs.append(raised / jnp.sum(raised, axis=-1, keepdims=True))
    return probs


def score_grad(probs, dprobs):
    cols = probs[0].shape[1]
    parts = []
    for h, prob in enumerate(probs):
        dpart = dprobs[:, h * cols : (h + 1) * cols]
        inner = jnp.sum(prob * dpart, axis=-1, keepdims=True)
        parts.append((prob * (dpart - inner) * SCALE).astype(BF))
    return jnp.concatenate(parts, axis=1)


def rounded(probs):
    return jnp.concatenate([p.astype(BF) for p in probs], axis=1)


PAIRS = 4


def spatial_fwd_kernel(q_ref, k_ref, v_ref, out_ref):
    for pair in range(PAIRS):
        cols = slice(pair * LANE, (pair + 1) * LANE)
        probs = soft(dot_nt(q_ref[:, cols], spread(k_ref[:, cols], 2)), 2)
        out_ref[:, cols] = dot_nn(rounded(probs), spread(v_ref[:, cols], 2)).astype(BF)


def spatial_fwd(q, k, v):
    spec = pl.BlockSpec((TOK, PAIRS * LANE), lambda i: (0, i))
    return pl.pallas_call(
        spatial_fwd_kernel,
        grid=(WIDTH // (PAIRS * LANE),),
        in_specs=[spec] * 3,
        out_specs=spec,
        out_shape=jax.ShapeDtypeStruct((TOK, WIDTH), BF),
        compiler_params=params(VMEM_MOST),
        name="spatial_fwd",
        cost_estimate=cost(4),
    )(q, k, v)


def spatial_bwd_kernel(gi_ref, w_ref, q_ref, k_ref, v_ref, dq_ref, dk_ref, dv_ref):
    dmixed = dot_nn(gi_ref[...], w_ref[...]).astype(BF)
    for pair in range(PAIRS):
        cols = slice(pair * LANE, (pair + 1) * LANE)
        q, dout = q_ref[:, cols], dmixed[:, cols]
        keys, values = spread(k_ref[:, cols], 2), spread(v_ref[:, cols], 2)
        probs = soft(dot_nt(q, keys), 2)
        dscores = score_grad(probs, dot_nt(dout, values))
        dv_ref[:, cols] = pick(dot_tn(rounded(probs), dout), 2).astype(BF)
        dq_ref[:, cols] = dot_nn(dscores, keys).astype(BF)
        dk_ref[:, cols] = pick(dot_tn(dscores, q), 2).astype(BF)


def spatial_bwd(grad_input, whole_out, q, k, v):
    spec = pl.BlockSpec((TOK, PAIRS * LANE), lambda i: (0, i))
    return pl.pallas_call(
        spatial_bwd_kernel,
        grid=(WIDTH // (PAIRS * LANE),),
        in_specs=[
            pl.BlockSpec((TOK, WIDTH), lambda i: (0, 0)),
            pl.BlockSpec((WIDTH, PAIRS * LANE), lambda i: (0, i)),
        ]
        + [spec] * 3,
        out_specs=[spec] * 3,
        out_shape=[jax.ShapeDtypeStruct((TOK, WIDTH), BF)] * 3,
        compiler_params=params(),
        name="spatial_bwd",
        cost_estimate=cost(9),
    )(grad_input, whole_out, q, k, v)


OUT_BLOCK = 512


PADDED = 256
THREE = 3 * PADDED


def widen(block, out_ref):
    for j in range(3):
        for h in range(3):
            out_ref[:, j * PADDED + h * HDIM : j * PADDED + (h + 1) * HDIM] = block[
                :, (h * 3 + j) * HDIM : (h * 3 + j + 1) * HDIM
            ]
        out_ref[:, j * PADDED + GROUP : (j + 1) * PADDED] = jnp.zeros(
            (block.shape[0], PADDED - GROUP), BF
        )


def out_norm_kernel(mixed_ref, w_ref, in_ref, gain_ref, hidden_ref, normed_ref, wide_ref):
    step = pl.program_id(0)
    block = in_ref[...].astype(F32) + dot_nt(mixed_ref[...], w_ref[:, :WIDTH])
    start = pl.multiple_of(step * OUT_BLOCK, OUT_BLOCK)
    hidden_ref[:, pl.ds(start, OUT_BLOCK)] = block.astype(BF)
    widen(w_ref[:, WIDTH:], wide_ref)

    @pl.when(step == pl.num_programs(0) - 1)
    def _():
        wide = hidden_ref[...].astype(F32)
        inverse = lax.rsqrt(jnp.mean(wide * wide, axis=-1, keepdims=True) + EPSILON)
        normed_ref[...] = (wide * inverse * gain_ref[...]).astype(BF)


def out_norm(mixed, weights, inputs, gain):
    whole = pl.BlockSpec((TOK, WIDTH), lambda i: (0, 0))
    return pl.pallas_call(
        out_norm_kernel,
        grid=(WIDTH // OUT_BLOCK,),
        in_specs=[
            whole,
            pl.BlockSpec((OUT_BLOCK, weights.shape[1]), lambda i: (i, 0)),
            pl.BlockSpec((TOK, OUT_BLOCK), lambda i: (0, i)),
            pl.BlockSpec((1, WIDTH), lambda i: (0, 0)),
        ],
        out_specs=[whole, whole, pl.BlockSpec((OUT_BLOCK, THREE), lambda i: (i, 0))],
        out_shape=[jax.ShapeDtypeStruct((TOK, WIDTH), BF)] * 2
        + [jax.ShapeDtypeStruct((WIDTH, THREE), BF)],
        compiler_params=params(VMEM_MOST),
        name="out_norm",
        cost_estimate=cost(5),
    )(mixed, weights, inputs, gain)


POS = 16
CHAINS = 8


def temporal_block(q, keys, values, dout, valid):
    keys, values = spread(keys, 3), spread(values, 3)
    probs = soft(dot_nt(q, keys), 3, valid)
    prob_round = rounded(probs)
    dscores = score_grad(probs, dot_nt(dout, values))
    return dot_nn(prob_round, values).astype(BF), (
        dot_nn(dscores, keys).astype(BF),
        pick(dot_tn(dscores, q), 3).astype(BF),
        pick(dot_tn(prob_round, dout), 3).astype(BF),
    )


def temporal_kernel(order_ref, *refs):
    proj, (grad_ref, out_ref, dproj_ref) = refs[:SEQ], refs[SEQ:]
    shape = (SEQ * POS, SEQ * POS)
    valid = (
        lax.broadcasted_iota(jnp.int32, shape, 0) % POS
        == lax.broadcasted_iota(jnp.int32, shape, 1) % POS
    )
    for chain in range(CHAINS):
        place = slice(chain * POS, (chain + 1) * POS)

        def rows(j):
            return jnp.concatenate(
                [p[place, j * PADDED : j * PADDED + GROUP] for p in proj], axis=0
            )

        dout = jnp.concatenate([grad_ref[order_ref[r], place] for r in range(SEQ)], axis=0)
        heads_out, grads = temporal_block(rows(0), rows(1), rows(2), dout, valid)
        for r in range(SEQ):
            here = slice(r * POS, (r + 1) * POS)
            out_ref[order_ref[r], place] = heads_out[here]
            for j in range(3):
                dproj_ref[r, place, j * PADDED : j * PADDED + GROUP] = grads[j][here]
                dproj_ref[r, place, j * PADDED + GROUP : (j + 1) * PADDED] = jnp.zeros(
                    (POS, PADDED - GROUP), BF
                )


def temporal(order, proj, grad_heads):
    rows = CHAINS * POS
    frame = pl.BlockSpec((rows, THREE), lambda i, o: (i, 0))
    heads = pl.BlockSpec((SEQ, rows, GROUP), lambda i, o: (0, i, 0))
    return pl.pallas_call(
        temporal_kernel,
        grid_spec=pltpu.PrefetchScalarGridSpec(
            num_scalar_prefetch=1,
            grid=(TOK // rows,),
            in_specs=[frame] * SEQ + [heads],
            out_specs=[heads, pl.BlockSpec((SEQ, rows, THREE), lambda i, o: (0, i, 0))],
        ),
        out_shape=[
            jax.ShapeDtypeStruct((SEQ, TOK, GROUP), BF),
            jax.ShapeDtypeStruct((SEQ, TOK, THREE), BF),
        ],
        compiler_params=params(),
        name="temporal",
        cost_estimate=cost(8),
    )(order, *proj, grad_heads)


SHARE_COLS = 512


def shares_kernel(dproj_ref, w_ref, *outs):
    left = dproj_ref[...].reshape(len(outs) * TOK, THREE)
    full = dot_nt(left, w_ref[...]).astype(BF)
    for r, out in enumerate(outs):
        out[...] = full[r * TOK : (r + 1) * TOK]


def shares_of(dproj, wide_proj, half):
    count = SEQ // 2
    return pl.pallas_call(
        shares_kernel,
        grid=(WIDTH // SHARE_COLS,),
        in_specs=[
            pl.BlockSpec((count, TOK, THREE), lambda i: (half, 0, 0)),
            pl.BlockSpec((SHARE_COLS, THREE), lambda i: (i, 0)),
        ],
        out_specs=[pl.BlockSpec((TOK, SHARE_COLS), lambda i: (0, i))] * count,
        out_shape=[jax.ShapeDtypeStruct((TOK, WIDTH), BF)] * count,
        compiler_params=params(),
        name="shares",
        cost_estimate=cost(2),
    )(dproj, wide_proj)


GRAD_ROWS = 512


def qkv_grad_kernel(factor, *refs):
    frames, dproj_ref, out_ref = refs[:-2], refs[-2], refs[-1]
    left = jnp.concatenate([f[...] for f in frames], axis=0)
    right = dproj_ref[...].reshape(SEQ * TOK, THREE)
    full = (dot_tn(left, right) * factor).astype(BF)
    for j in range(3):
        for h in range(3):
            out_ref[:, (h * 3 + j) * HDIM : (h * 3 + j + 1) * HDIM] = full[
                :, j * PADDED + h * HDIM : j * PADDED + (h + 1) * HDIM
            ]


def qkv_product(frames, dproj, factor):
    return pl.pallas_call(
        functools.partial(qkv_grad_kernel, factor),
        grid=(WIDTH // GRAD_ROWS,),
        in_specs=[pl.BlockSpec((f.shape[0], GRAD_ROWS), lambda i: (0, i)) for f in frames]
        + [pl.BlockSpec((SEQ, TOK, THREE), lambda i: (0, 0, 0))],
        out_specs=pl.BlockSpec((GRAD_ROWS, 3 * GROUP), lambda i: (i, 0)),
        out_shape=jax.ShapeDtypeStruct((WIDTH, 3 * GROUP), BF),
        compiler_params=params(),
        name="qkv_product",
        cost_estimate=cost(5),
    )(*frames, dproj)


SHARE = 12
SLOT = 16
FOUR = 4
EXTRA = 16
GROUPED = DP * SLOT


def mover():
    shape = (FOUR * SHARE * SEQ, FOUR * SLOT * SEQ)
    source = lax.broadcasted_iota(jnp.int32, shape, 0)
    target = lax.broadcasted_iota(jnp.int32, shape, 1)
    group = target // (FOUR * SLOT)
    block = (target // SLOT) % FOUR
    turn = target % SLOT
    wanted = block * (SHARE * SEQ) + group * SHARE + turn
    return jnp.where((source == wanted) & (turn < SHARE), 1.0, 0.0).astype(BF)


def two_parts(row):
    high = row.astype(BF)
    return high, (row - high.astype(F32)).astype(BF)


def grad_input_kernel(factor, sum_a, sum_b, sum_c, sum_d, hidden_ref, resid_ref, gain_ref,
                      heads_ref, out_ref, groups_ref):
    def wide(ref):
        return ref[...].astype(F32)

    dnormed = (wide(sum_a) + wide(sum_b) + wide(sum_c) + wide(sum_d)).astype(BF).astype(F32)
    hidden = wide(hidden_ref)
    inverse = lax.rsqrt(jnp.mean(hidden * hidden, axis=-1, keepdims=True) + EPSILON)
    unit = hidden * inverse
    gain_high, gain_low = two_parts(jnp.sum(dnormed * unit, axis=0, keepdims=True) * factor)
    scaled = dnormed * gain_ref[...]
    through = inverse * (scaled - unit * jnp.mean(scaled * unit, axis=-1, keepdims=True))
    grad = (wide(resid_ref) + through).astype(BF)
    out_ref[...] = grad
    row = lax.broadcasted_iota(jnp.int32, (EXTRA, WIDTH), 0)
    extra = jnp.where(row == 0, gain_high.astype(F32), jnp.where(row == 1, gain_low.astype(F32), 0.0))
    both = jnp.concatenate([grad, extra.astype(BF)], axis=0)
    move = mover()
    rows, cols = FOUR * SHARE * SEQ, FOUR * SLOT
    for four in range(DP // FOUR):
        moved = dot_nn(both[:, four * rows : (four + 1) * rows], move).astype(BF)
        for j in range(SEQ):
            groups_ref[j, :, four * cols : (four + 1) * cols] = moved[:, j * cols : (j + 1) * cols]
    groups_ref[:, :TOK, GROUPED:] = heads_ref[...]
    groups_ref[:, TOK:, GROUPED:] = jnp.zeros((SEQ, EXTRA, GROUP), BF)


def grad_input_call(sums, hidden, resid, gain, heads_out, factor):
    return pl.pallas_call(
        functools.partial(grad_input_kernel, factor),
        out_shape=[
            jax.ShapeDtypeStruct((TOK, WIDTH), BF),
            jax.ShapeDtypeStruct((SEQ, TOK + EXTRA, GROUPED + GROUP), BF),
        ],
        compiler_params=params(),
        name="grad_input",
        cost_estimate=cost(2),
    )(*sums, hidden, resid, gain, heads_out)


def out_product_kernel(factor, order_ref, groups_ref, mixed_ref, mine_ref, other_ref, turned):
    @pl.when(pl.program_id(0) == 0)
    def _():
        for r in range(SEQ):
            turned[:, r * TOK : (r + 1) * TOK] = groups_ref[order_ref[r], :TOK].T

    product = dot_nn(turned[...], mixed_ref[...]) * factor
    extras = sum(groups_ref[r, TOK:].astype(F32) for r in range(SEQ))
    high, low = two_parts(extras[0:1] + extras[1:2])
    turn = lax.broadcasted_iota(jnp.int32, (GROUPED, GROUPED), 0) % SLOT
    first = pl.program_id(0) == 0
    begin = product[:, :GROUPED]
    for place, part in ((SHARE, high), (SHARE + 1, low)):
        begin = jnp.where((turn == place) & first, part.astype(F32), begin)
    product = jnp.concatenate([begin, product[:, GROUPED:]], axis=1).astype(BF)
    first_core = order_ref[SEQ] == 0
    for d in range(DP // 2):
        even = product[2 * d * SLOT : (2 * d + 1) * SLOT]
        odd = product[(2 * d + 1) * SLOT : (2 * d + 2) * SLOT]
        mine_ref[d] = jnp.where(first_core, even, odd)
        other_ref[d] = jnp.where(first_core, odd, even)


def out_product(order, groups, mixed_all, factor):
    cols = 512
    spec = pl.BlockSpec((DP // 2, SLOT, cols), lambda i, o: (0, 0, i))
    return pl.pallas_call(
        functools.partial(out_product_kernel, factor),
        grid_spec=pltpu.PrefetchScalarGridSpec(
            num_scalar_prefetch=1,
            grid=(WIDTH // cols,),
            in_specs=[
                pl.BlockSpec((SEQ, TOK + EXTRA, GROUPED), lambda i, o: (0, 0, 0)),
                pl.BlockSpec((SEQ * TOK, cols), lambda i, o: (0, i)),
            ],
            out_specs=[spec, spec],
            scratch_shapes=[pltpu.VMEM((GROUPED, SEQ * TOK), BF)],
        ),
        out_shape=[jax.ShapeDtypeStruct((DP // 2, SLOT, WIDTH), BF)] * 2,
        compiler_params=params(),
        name="out_product",
        cost_estimate=cost(3),
    )(order, groups, mixed_all)


def fold_kernel(in_ref, out_ref):
    total = in_ref[0].astype(F32)
    for d in range(1, DP // 2):
        total = total + in_ref[d].astype(F32)
    high, low = two_parts(total[SHARE : SHARE + 1] + total[SHARE + 1 : SHARE + 2])
    turn = lax.broadcasted_iota(jnp.int32, total.shape, 0)
    total = jnp.where(turn == SHARE, high.astype(F32), total)
    total = jnp.where(turn == SHARE + 1, low.astype(F32), total).astype(BF)
    for j in range(SEQ):
        out_ref[j] = total


def fold(pieces):
    return pl.pallas_call(
        fold_kernel,
        out_shape=jax.ShapeDtypeStruct((SEQ, SLOT, WIDTH), BF),
        compiler_params=params(),
        name="fold",
        cost_estimate=cost(1.5),
    )(pieces)


def finish_kernel(in_ref, out_ref, gain_ref):
    out_ref[...] = jnp.concatenate(
        [in_ref[j].astype(F32)[:SHARE] for j in range(SEQ)], axis=0
    )
    move = mover()
    rows, cols = FOUR * SHARE * SEQ, FOUR * SLOT
    for four in range(DP // FOUR):
        left = jnp.concatenate(
            [in_ref[j, :, four * cols : (four + 1) * cols] for j in range(SEQ)], axis=1
        )
        back = dot_nt(left, move)
        gain_ref[pl.ds(four * rows, rows)] = back[SHARE] + back[SHARE + 1]


def finish(gathered):
    return pl.pallas_call(
        finish_kernel,
        out_shape=[
            jax.ShapeDtypeStruct((SEQ * SHARE, WIDTH), F32),
            jax.ShapeDtypeStruct((WIDTH,), F32),
        ],
        compiler_params=params(),
        name="finish",
        cost_estimate=cost(2),
    )(gathered)


def along_x(array, shift):
    pairs = [(i, ((i // 2 + shift) % XS) * 2 + i % 2) for i in range(SEQ)]
    return lax.ppermute(array, "seq", pairs)


def across_y(array):
    return lax.ppermute(array, "seq", [(i, i ^ 1) for i in range(SEQ)])


HALF = TOK // 2


def gather_frames(own):
    behind, ahead, partner = along_x(own, 1), along_x(own, -1), across_y(own)
    far_top, far_low = along_x(behind[:HALF], 1), along_x(ahead[HALF:], -1)
    partner_behind, partner_ahead = along_x(partner, 1), along_x(partner, -1)
    return (
        own, behind, ahead, far_top, far_low,
        partner, partner_behind, partner_ahead, across_y(far_top), across_y(far_low),
    )


def gather_by_x(own):
    partner, behind, ahead, far = across_y(own), along_x(own, 1), along_x(own, -1), along_x(own, 2)
    return (
        own, behind, ahead, far,
        partner, along_x(partner, 1), along_x(partner, -1), along_x(partner, 2),
    )


def whole_frames(parts):
    own, behind, ahead, top, low, partner, pbehind, pahead, ptop, plow = parts
    return (
        own, behind, ahead, jnp.concatenate([top, low], axis=0),
        partner, pbehind, pahead, jnp.concatenate([ptop, plow], axis=0),
    )


def scatter_frames(own, behind, ahead, far, partner, from_pbehind, from_pahead):
    partner = partner + from_pbehind + from_pahead
    top, low = along_x(far[:HALF], -1), along_x(far[HALF:], 1)
    behind = jnp.concatenate([behind[:HALF] + top, behind[HALF:]], axis=0)
    ahead = jnp.concatenate([ahead[:HALF], ahead[HALF:] + low], axis=0)
    return own, across_y(partner), along_x(behind, -1), along_x(ahead, 1)


def settle_kernel(in_ref, out_ref):
    out_ref[...] = in_ref[...]


def settle(array):
    return pl.pallas_call(
        settle_kernel,
        out_shape=jax.ShapeDtypeStruct(array.shape, array.dtype),
        compiler_params=params(),
        name="settle",
        cost_estimate=cost(1),
    )(array)


def beside_kernel(a_ref, b_ref, out_ref):
    out_ref[:, : a_ref.shape[1]] = a_ref[...]
    out_ref[:, a_ref.shape[1] :] = b_ref[...]


def beside(a, b):
    return pl.pallas_call(
        beside_kernel,
        out_shape=jax.ShapeDtypeStruct((a.shape[0], a.shape[1] + b.shape[1]), a.dtype),
        compiler_params=params(VMEM_MOST),
        name="beside",
        cost_estimate=cost(1),
    )(a, b)


def chip_exchange(blocks):
    groups = [[2 * i + c for i in range(DP // 2)] for c in range(2)]
    return lax.all_to_all(blocks, "dp", 0, 0, axis_index_groups=groups, tiled=True)


def body(
    inputs, spatial_q, spatial_k, spatial_v, out_weight, norm_gain, qkv_weight, grad_out, grad_resid
):
    block_shape = inputs.shape
    factor = (TOK * DP * SEQ) ** (-0.5)
    flat_in, q, k, v, dout, resid = (
        a.reshape(TOK, WIDTH)
        for a in (inputs, spatial_q, spatial_k, spatial_v, grad_out, grad_resid)
    )
    gain = norm_gain.reshape(1, WIDTH)
    me = lax.axis_index("seq")
    place_x, place_y = me // 2, me % 2
    order = jnp.stack(
        [((place_x + s) % XS) * 2 + y for y in (place_y, 1 - place_y) for s in (0, 3, 1, 2)]
        + [lax.axis_index("dp") % 2]
    ).astype(jnp.int32)

    weights = lax.all_gather(
        beside(out_weight, qkv_weight), "dp", axis=0, tiled=True
    )
    mixed = spatial_fwd(q, k, v)
    grad_heads = settle(
        lax.all_to_all(
            dout.reshape(TOK, SEQ, GROUP).transpose(1, 0, 2), "seq", 0, 0, tiled=True
        )
    )
    mixed_parts = gather_by_x(mixed)
    mixed_all = jnp.concatenate(mixed_parts, axis=0)
    weights, grad_heads, mixed_all = lax.optimization_barrier((weights, grad_heads, mixed_all))
    hidden, normed, wide_proj = out_norm(mixed, weights, flat_in, gain)
    normed_parts = gather_frames(normed)
    proj = [dot_nn(f, wide_proj).astype(BF) for f in whole_frames(normed_parts)]
    heads_out, dproj = temporal(order, proj, grad_heads)
    partner, pbehind, pahead, pfar = shares_of(dproj, wide_proj, 1)
    partner, pbehind, pahead, pfar, dproj = lax.optimization_barrier(
        (partner, pbehind, pahead, pfar, dproj)
    )
    qkv_share = qkv_product(normed_parts, dproj, factor)
    qkv_grad = lax.psum_scatter(qkv_share, "dp", scatter_dimension=0, tiled=True)
    pfar, pbehind, pahead = lax.optimization_barrier(
        (across_y(pfar), along_x(pbehind, -1), along_x(pahead, 1))
    )
    own, behind, ahead, far = shares_of(dproj, wide_proj, 0)
    sums = scatter_frames(own, behind, ahead, far + pfar, partner, pbehind, pahead)

    grad_input, groups = grad_input_call(sums, hidden, resid, gain, heads_out, factor)
    groups = lax.all_to_all(groups, "seq", 0, 0, tiled=True)
    grads = spatial_bwd(grad_input, weights, q, k, v)
    groups, *grads = lax.optimization_barrier((groups, *grads))
    mine, other = out_product(order, groups, mixed_all, factor)
    summed = mine + lax.ppermute(other, "dp", [(i, i ^ 1) for i in range(DP)])
    received = chip_exchange(summed)
    temporal_out = groups[:, :TOK, GROUPED:].transpose(1, 0, 2).reshape(TOK, WIDTH)
    gathered = lax.all_to_all(fold(received), "seq", 0, 0, tiled=True)
    gathered, qkv_grad = lax.optimization_barrier((gathered, qkv_grad.astype(F32)))
    out_grad, gain_grad = finish(gathered)
    return tuple(a.reshape(block_shape) for a in (hidden, temporal_out, grad_input, *grads)) + (
        qkv_grad,
        out_grad,
        gain_grad,
    )


def solution(mesh):
    tokens = P("dp", "seq", None, None, None)
    return jax.shard_map(
        body,
        mesh=mesh,
        in_specs=(
            tokens, tokens, tokens, tokens, P("dp", None), P(), P("dp", "seq"), tokens, tokens,
        ),
        out_specs=(
            tokens, tokens, tokens, tokens, tokens, tokens, P("dp", "seq"), P("dp", None), P(),
        ),
        check_vma=False,
    )
```

```python
import functools

import jax
import jax.numpy as jnp
from jax import lax
from jax.experimental import pallas as pl
from jax.experimental.pallas import tpu as pltpu
from jax.sharding import PartitionSpec as P

HEADS = 24
HDIM = 64
EPSILON = 1e-06
XS = 4
SEQ = 8
DP = 16
TOK = 128
WIDTH = HEADS * HDIM
GROUP = WIDTH // SEQ
LANE = 128
BF = jnp.bfloat16
F32 = jnp.float32
SCALE = HDIM**-0.5
VMEM_LIMIT = 20 * 1024 * 1024
VMEM_MOST = 58 * 1024 * 1024
HBM_RATE = 3_000_000


def params(limit=VMEM_LIMIT):
    return pltpu.CompilerParams(vmem_limit_bytes=limit)


def cost(micros):
    return pl.CostEstimate(flops=0, bytes_accessed=int(micros * HBM_RATE), transcendentals=0)


def dot_nt(a, b):
    return lax.dot_general(a, b, (((1,), (1,)), ((), ())), preferred_element_type=F32)


def dot_tn(a, b):
    return lax.dot_general(a, b, (((0,), (0,)), ((), ())), preferred_element_type=F32)


def dot_nn(a, b):
    return lax.dot_general(a, b, (((1,), (0,)), ((), ())), preferred_element_type=F32)


def spread(block, heads):
    lane = lax.broadcasted_iota(jnp.int32, block.shape, 1) // HDIM
    return jnp.concatenate(
        [jnp.where(lane == h, block, jnp.zeros_like(block)) for h in range(heads)], axis=0
    )


def pick(stacked, heads):
    rows = stacked.shape[0] // heads
    lane = lax.broadcasted_iota(jnp.int32, (rows, stacked.shape[1]), 1) // HDIM
    out = stacked[:rows]
    for h in range(1, heads):
        out = jnp.where(lane == h, stacked[h * rows : (h + 1) * rows], out)
    return out


def soft(scores, heads, valid=None):
    cols = scores.shape[1] // heads
    probs = []
    for h in range(heads):
        part = scores[:, h * cols : (h + 1) * cols] * SCALE
        if valid is not None:
            part = jnp.where(valid, part, -jnp.inf)
        raised = jnp.exp(part - jnp.max(part, axis=-1, keepdims=True))
        probs.append(raised / jnp.sum(raised, axis=-1, keepdims=True))
    return probs


def score_grad(probs, dprobs):
    cols = probs[0].shape[1]
    parts = []
    for h, prob in enumerate(probs):
        dpart = dprobs[:, h * cols : (h + 1) * cols]
        inner = jnp.sum(prob * dpart, axis=-1, keepdims=True)
        parts.append((prob * (dpart - inner) * SCALE).astype(BF))
    return jnp.concatenate(parts, axis=1)


def rounded(probs):
    return jnp.concatenate([p.astype(BF) for p in probs], axis=1)


PAIRS = 4


def spatial_fwd_kernel(q_ref, k_ref, v_ref, out_ref):
    for pair in range(PAIRS):
        cols = slice(pair * LANE, (pair + 1) * LANE)
        probs = soft(dot_nt(q_ref[:, cols], spread(k_ref[:, cols], 2)), 2)
        out_ref[:, cols] = dot_nn(rounded(probs), spread(v_ref[:, cols], 2)).astype(BF)


def spatial_fwd(q, k, v):
    spec = pl.BlockSpec((TOK, PAIRS * LANE), lambda i: (0, i))
    return pl.pallas_call(
        spatial_fwd_kernel,
        grid=(WIDTH // (PAIRS * LANE),),
        in_specs=[spec] * 3,
        out_specs=spec,
        out_shape=jax.ShapeDtypeStruct((TOK, WIDTH), BF),
        compiler_params=params(VMEM_MOST),
        name="spatial_fwd",
        cost_estimate=cost(4),
    )(q, k, v)


def spatial_bwd_kernel(gi_ref, w_ref, q_ref, k_ref, v_ref, dq_ref, dk_ref, dv_ref):
    dmixed = dot_nn(gi_ref[...], w_ref[...]).astype(BF)
    for pair in range(PAIRS):
        cols = slice(pair * LANE, (pair + 1) * LANE)
        q, dout = q_ref[:, cols], dmixed[:, cols]
        keys, values = spread(k_ref[:, cols], 2), spread(v_ref[:, cols], 2)
        probs = soft(dot_nt(q, keys), 2)
        dscores = score_grad(probs, dot_nt(dout, values))
        dv_ref[:, cols] = pick(dot_tn(rounded(probs), dout), 2).astype(BF)
        dq_ref[:, cols] = dot_nn(dscores, keys).astype(BF)
        dk_ref[:, cols] = pick(dot_tn(dscores, q), 2).astype(BF)


def spatial_bwd(grad_input, whole_out, q, k, v):
    spec = pl.BlockSpec((TOK, PAIRS * LANE), lambda i: (0, i))
    return pl.pallas_call(
        spatial_bwd_kernel,
        grid=(WIDTH // (PAIRS * LANE),),
        in_specs=[
            pl.BlockSpec((TOK, WIDTH), lambda i: (0, 0)),
            pl.BlockSpec((WIDTH, PAIRS * LANE), lambda i: (0, i)),
        ]
        + [spec] * 3,
        out_specs=[spec] * 3,
        out_shape=[jax.ShapeDtypeStruct((TOK, WIDTH), BF)] * 3,
        compiler_params=params(VMEM_MOST),
        name="spatial_bwd",
        cost_estimate=cost(9),
    )(grad_input, whole_out, q, k, v)


OUT_BLOCK = 512


PADDED = 256
THREE = 3 * PADDED


def widen(block, out_ref):
    for j in range(3):
        for h in range(3):
            out_ref[:, j * PADDED + h * HDIM : j * PADDED + (h + 1) * HDIM] = block[
                :, (h * 3 + j) * HDIM : (h * 3 + j + 1) * HDIM
            ]
        out_ref[:, j * PADDED + GROUP : (j + 1) * PADDED] = jnp.zeros(
            (block.shape[0], PADDED - GROUP), BF
        )


def out_norm_kernel(mixed_ref, w_ref, in_ref, gain_ref, hidden_ref, normed_ref, wide_ref):
    step = pl.program_id(0)
    block = in_ref[...].astype(F32) + dot_nt(mixed_ref[...], w_ref[:, :WIDTH])
    start = pl.multiple_of(step * OUT_BLOCK, OUT_BLOCK)
    hidden_ref[:, pl.ds(start, OUT_BLOCK)] = block.astype(BF)
    widen(w_ref[:, WIDTH:], wide_ref)

    @pl.when(step == pl.num_programs(0) - 1)
    def _():
        wide = hidden_ref[...].astype(F32)
        inverse = lax.rsqrt(jnp.mean(wide * wide, axis=-1, keepdims=True) + EPSILON)
        normed_ref[...] = (wide * inverse * gain_ref[...]).astype(BF)


def out_norm(mixed, weights, inputs, gain):
    whole = pl.BlockSpec((TOK, WIDTH), lambda i: (0, 0))
    return pl.pallas_call(
        out_norm_kernel,
        grid=(WIDTH // OUT_BLOCK,),
        in_specs=[
            whole,
            pl.BlockSpec((OUT_BLOCK, weights.shape[1]), lambda i: (i, 0)),
            pl.BlockSpec((TOK, OUT_BLOCK), lambda i: (0, i)),
            pl.BlockSpec((1, WIDTH), lambda i: (0, 0)),
        ],
        out_specs=[whole, whole, pl.BlockSpec((OUT_BLOCK, THREE), lambda i: (i, 0))],
        out_shape=[jax.ShapeDtypeStruct((TOK, WIDTH), BF)] * 2
        + [jax.ShapeDtypeStruct((WIDTH, THREE), BF)],
        compiler_params=params(VMEM_MOST),
        name="out_norm",
        cost_estimate=cost(5),
    )(mixed, weights, inputs, gain)


POS = 16
CHAINS = 8


def temporal_block(q, keys, values, dout, valid):
    keys, values = spread(keys, 3), spread(values, 3)
    probs = soft(dot_nt(q, keys), 3, valid)
    prob_round = rounded(probs)
    dscores = score_grad(probs, dot_nt(dout, values))
    return dot_nn(prob_round, values).astype(BF), (
        dot_nn(dscores, keys).astype(BF),
        pick(dot_tn(dscores, q), 3).astype(BF),
        pick(dot_tn(prob_round, dout), 3).astype(BF),
    )


def temporal_kernel(order_ref, *refs):
    proj, (grad_ref, out_ref, dproj_ref) = refs[:SEQ], refs[SEQ:]
    shape = (SEQ * POS, SEQ * POS)
    valid = (
        lax.broadcasted_iota(jnp.int32, shape, 0) % POS
        == lax.broadcasted_iota(jnp.int32, shape, 1) % POS
    )
    for chain in range(CHAINS):
        place = slice(chain * POS, (chain + 1) * POS)

        def rows(j):
            return jnp.concatenate(
                [p[place, j * PADDED : j * PADDED + GROUP] for p in proj], axis=0
            )

        dout = jnp.concatenate([grad_ref[order_ref[r], place] for r in range(SEQ)], axis=0)
        heads_out, grads = temporal_block(rows(0), rows(1), rows(2), dout, valid)
        for r in range(SEQ):
            here = slice(r * POS, (r + 1) * POS)
            out_ref[order_ref[r], place] = heads_out[here]
            for j in range(3):
                dproj_ref[r, place, j * PADDED : j * PADDED + GROUP] = grads[j][here]
                dproj_ref[r, place, j * PADDED + GROUP : (j + 1) * PADDED] = jnp.zeros(
                    (POS, PADDED - GROUP), BF
                )


def temporal(order, proj, grad_heads):
    rows = CHAINS * POS
    frame = pl.BlockSpec((rows, THREE), lambda i, o: (i, 0))
    heads = pl.BlockSpec((SEQ, rows, GROUP), lambda i, o: (0, i, 0))
    return pl.pallas_call(
        temporal_kernel,
        grid_spec=pltpu.PrefetchScalarGridSpec(
            num_scalar_prefetch=1,
            grid=(TOK // rows,),
            in_specs=[frame] * SEQ + [heads],
            out_specs=[heads, pl.BlockSpec((SEQ, rows, THREE), lambda i, o: (0, i, 0))],
        ),
        out_shape=[
            jax.ShapeDtypeStruct((SEQ, TOK, GROUP), BF),
            jax.ShapeDtypeStruct((SEQ, TOK, THREE), BF),
        ],
        compiler_params=params(),
        name="temporal",
        cost_estimate=cost(8),
    )(order, *proj, grad_heads)


SHARE_COLS = 512


def shares_kernel(dproj_ref, w_ref, *outs):
    left = dproj_ref[...].reshape(len(outs) * TOK, THREE)
    full = dot_nt(left, w_ref[...]).astype(BF)
    for r, out in enumerate(outs):
        out[...] = full[r * TOK : (r + 1) * TOK]


def shares_of(dproj, wide_proj, half):
    count = SEQ // 2
    return pl.pallas_call(
        shares_kernel,
        grid=(WIDTH // SHARE_COLS,),
        in_specs=[
            pl.BlockSpec((count, TOK, THREE), lambda i: (half, 0, 0)),
            pl.BlockSpec((SHARE_COLS, THREE), lambda i: (i, 0)),
        ],
        out_specs=[pl.BlockSpec((TOK, SHARE_COLS), lambda i: (0, i))] * count,
        out_shape=[jax.ShapeDtypeStruct((TOK, WIDTH), BF)] * count,
        compiler_params=params(),
        name="shares",
        cost_estimate=cost(2),
    )(dproj, wide_proj)


GRAD_ROWS = 512


def qkv_grad_kernel(factor, *refs):
    frames, dproj_ref, out_ref = refs[:-2], refs[-2], refs[-1]
    left = jnp.concatenate([f[...] for f in frames], axis=0)
    right = dproj_ref[...].reshape(SEQ * TOK, THREE)
    full = (dot_tn(left, right) * factor).astype(BF)
    for j in range(3):
        for h in range(3):
            out_ref[:, (h * 3 + j) * HDIM : (h * 3 + j + 1) * HDIM] = full[
                :, j * PADDED + h * HDIM : j * PADDED + (h + 1) * HDIM
            ]


def qkv_product(frames, dproj, factor):
    return pl.pallas_call(
        functools.partial(qkv_grad_kernel, factor),
        grid=(WIDTH // GRAD_ROWS,),
        in_specs=[pl.BlockSpec((f.shape[0], GRAD_ROWS), lambda i: (0, i)) for f in frames]
        + [pl.BlockSpec((SEQ, TOK, THREE), lambda i: (0, 0, 0))],
        out_specs=pl.BlockSpec((GRAD_ROWS, 3 * GROUP), lambda i: (i, 0)),
        out_shape=jax.ShapeDtypeStruct((WIDTH, 3 * GROUP), BF),
        compiler_params=params(),
        name="qkv_product",
        cost_estimate=cost(5),
    )(*frames, dproj)


SHARE = 12
SLOT = 16
FOUR = 4
EXTRA = 16
GROUPED = DP * SHARE


def mover():
    size = FOUR * SHARE * SEQ
    source = lax.broadcasted_iota(jnp.int32, (size, size), 0)
    target = lax.broadcasted_iota(jnp.int32, (size, size), 1)
    group = target // (FOUR * SHARE)
    block = (target // SHARE) % FOUR
    wanted = block * (SHARE * SEQ) + group * SHARE + target % SHARE
    return jnp.where(source == wanted, 1.0, 0.0).astype(BF)


def two_parts(row):
    high = row.astype(BF)
    return high, (row - high.astype(F32)).astype(BF)


def grad_input_kernel(factor, sum_a, sum_b, sum_c, sum_d, hidden_ref, resid_ref, gain_ref,
                      heads_ref, out_ref, groups_ref):
    def wide(ref):
        return ref[...].astype(F32)

    dnormed = (wide(sum_a) + wide(sum_b) + wide(sum_c) + wide(sum_d)).astype(BF).astype(F32)
    hidden = wide(hidden_ref)
    inverse = lax.rsqrt(jnp.mean(hidden * hidden, axis=-1, keepdims=True) + EPSILON)
    unit = hidden * inverse
    gain_high, gain_low = two_parts(jnp.sum(dnormed * unit, axis=0, keepdims=True) * factor)
    scaled = dnormed * gain_ref[...]
    through = inverse * (scaled - unit * jnp.mean(scaled * unit, axis=-1, keepdims=True))
    grad = (wide(resid_ref) + through).astype(BF)
    out_ref[...] = grad
    row = lax.broadcasted_iota(jnp.int32, (EXTRA, WIDTH), 0)
    extra = jnp.where(row == 0, gain_high.astype(F32), jnp.where(row == 1, gain_low.astype(F32), 0.0))
    both = jnp.concatenate([grad, extra.astype(BF)], axis=0)
    move = mover()
    rows, cols = FOUR * SHARE * SEQ, FOUR * SHARE
    for four in range(DP // FOUR):
        moved = dot_nn(both[:, four * rows : (four + 1) * rows], move).astype(BF)
        for j in range(SEQ):
            groups_ref[j, :, four * cols : (four + 1) * cols] = moved[:, j * cols : (j + 1) * cols]
    groups_ref[:, :TOK, GROUPED:] = heads_ref[...]
    groups_ref[:, TOK:, GROUPED:] = jnp.zeros((SEQ, EXTRA, GROUP), BF)


def grad_input_call(sums, hidden, resid, gain, heads_out, factor):
    return pl.pallas_call(
        functools.partial(grad_input_kernel, factor),
        out_shape=[
            jax.ShapeDtypeStruct((TOK, WIDTH), BF),
            jax.ShapeDtypeStruct((SEQ, TOK + EXTRA, GROUPED + GROUP), BF),
        ],
        compiler_params=params(),
        name="grad_input",
        cost_estimate=cost(2),
    )(*sums, hidden, resid, gain, heads_out)


def out_product_kernel(factor, order_ref, groups_ref, mixed_ref, mine_ref, other_ref, turned):
    @pl.when(pl.program_id(0) == 0)
    def _():
        for r in range(SEQ):
            turned[:, r * TOK : (r + 1) * TOK] = groups_ref[order_ref[r], :TOK, :GROUPED].T

    product = dot_nn(turned[...], mixed_ref[...]) * factor
    cols = product.shape[1]
    extras = sum(groups_ref[r, TOK:, :GROUPED].astype(F32) for r in range(SEQ))
    gain_parts = jnp.concatenate(
        [part.astype(F32) for part in two_parts(extras[0:1] + extras[1:2])], axis=0
    )
    gain_parts = jnp.concatenate([gain_parts, jnp.zeros((2, cols - GROUPED), F32)], axis=1)
    gain_parts = jnp.where(pl.program_id(0) == 0, gain_parts, 0.0)
    tail = jnp.concatenate([gain_parts, jnp.zeros((SLOT - SHARE - 2, cols), F32)], axis=0)

    def block(d):
        return jnp.concatenate([product[d * SHARE : (d + 1) * SHARE], tail], axis=0).astype(BF)

    first_core = order_ref[SEQ] == 0
    for d in range(DP // 2):
        even, odd = block(2 * d), block(2 * d + 1)
        mine_ref[d] = jnp.where(first_core, even, odd)
        other_ref[d] = jnp.where(first_core, odd, even)


def out_product(order, groups, mixed_all, factor):
    cols = 512
    spec = pl.BlockSpec((DP // 2, SLOT, cols), lambda i, o: (0, 0, i))
    return pl.pallas_call(
        functools.partial(out_product_kernel, factor),
        grid_spec=pltpu.PrefetchScalarGridSpec(
            num_scalar_prefetch=1,
            grid=(WIDTH // cols,),
            in_specs=[
                pl.BlockSpec(groups.shape, lambda i, o: (0, 0, 0)),
                pl.BlockSpec((SEQ * TOK, cols), lambda i, o: (0, i)),
            ],
            out_specs=[spec, spec],
            scratch_shapes=[pltpu.VMEM((GROUPED, SEQ * TOK), BF)],
        ),
        out_shape=[jax.ShapeDtypeStruct((DP // 2, SLOT, WIDTH), BF)] * 2,
        compiler_params=params(),
        name="out_product",
        cost_estimate=cost(3),
    )(order, groups, mixed_all)


def fold_kernel(in_ref, out_ref):
    total = in_ref[0].astype(F32)
    for d in range(1, DP // 2):
        total = total + in_ref[d].astype(F32)
    high, low = two_parts(total[SHARE : SHARE + 1] + total[SHARE + 1 : SHARE + 2])
    turn = lax.broadcasted_iota(jnp.int32, total.shape, 0)
    total = jnp.where(turn == SHARE, high.astype(F32), total)
    total = jnp.where(turn == SHARE + 1, low.astype(F32), total).astype(BF)
    for j in range(SEQ):
        out_ref[j] = total


def fold(pieces):
    return pl.pallas_call(
        fold_kernel,
        out_shape=jax.ShapeDtypeStruct((SEQ, SLOT, WIDTH), BF),
        compiler_params=params(),
        name="fold",
        cost_estimate=cost(1.5),
    )(pieces)


def finish_kernel(in_ref, out_ref, gain_ref):
    out_ref[...] = jnp.concatenate(
        [in_ref[j].astype(F32)[:SHARE] for j in range(SEQ)], axis=0
    )
    move = mover()
    rows, cols = FOUR * SHARE * SEQ, FOUR * SHARE
    for four in range(DP // FOUR):
        left = jnp.concatenate(
            [in_ref[j, :, four * cols : (four + 1) * cols] for j in range(SEQ)], axis=1
        )
        back = dot_nt(left, move)
        gain_ref[pl.ds(four * rows, rows)] = back[SHARE] + back[SHARE + 1]


def finish(gathered):
    return pl.pallas_call(
        finish_kernel,
        out_shape=[
            jax.ShapeDtypeStruct((SEQ * SHARE, WIDTH), F32),
            jax.ShapeDtypeStruct((WIDTH,), F32),
        ],
        compiler_params=params(),
        name="finish",
        cost_estimate=cost(2),
    )(gathered)


def along_x(array, shift):
    pairs = [(i, ((i // 2 + shift) % XS) * 2 + i % 2) for i in range(SEQ)]
    return lax.ppermute(array, "seq", pairs)


def across_y(array):
    return lax.ppermute(array, "seq", [(i, i ^ 1) for i in range(SEQ)])


HALF = TOK // 2


def gather_frames(own):
    behind, ahead, partner = along_x(own, 1), along_x(own, -1), across_y(own)
    far_top, far_low = along_x(behind[:HALF], 1), along_x(ahead[HALF:], -1)
    partner_behind, partner_ahead = along_x(partner, 1), along_x(partner, -1)
    return (
        own, behind, ahead, far_top, far_low,
        partner, partner_behind, partner_ahead, across_y(far_top), across_y(far_low),
    )


def gather_by_x(own):
    partner, behind, ahead, far = across_y(own), along_x(own, 1), along_x(own, -1), along_x(own, 2)
    return (
        own, behind, ahead, far,
        partner, along_x(partner, 1), along_x(partner, -1), along_x(partner, 2),
    )


def whole_frames(parts):
    own, behind, ahead, top, low, partner, pbehind, pahead, ptop, plow = parts
    return (
        own, behind, ahead, jnp.concatenate([top, low], axis=0),
        partner, pbehind, pahead, jnp.concatenate([ptop, plow], axis=0),
    )


def scatter_frames(own, behind, ahead, far, partner, from_pbehind, from_pahead):
    partner = partner + from_pbehind + from_pahead
    top, low = along_x(far[:HALF], -1), along_x(far[HALF:], 1)
    behind = jnp.concatenate([behind[:HALF] + top, behind[HALF:]], axis=0)
    ahead = jnp.concatenate([ahead[:HALF], ahead[HALF:] + low], axis=0)
    return own, across_y(partner), along_x(behind, -1), along_x(ahead, 1)


def settle_kernel(in_ref, out_ref):
    out_ref[...] = in_ref[...]


def settle(array):
    return pl.pallas_call(
        settle_kernel,
        out_shape=jax.ShapeDtypeStruct(array.shape, array.dtype),
        compiler_params=params(),
        name="settle",
        cost_estimate=cost(1),
    )(array)


def beside_kernel(a_ref, b_ref, out_ref):
    out_ref[:, : a_ref.shape[1]] = a_ref[...]
    out_ref[:, a_ref.shape[1] :] = b_ref[...]


def beside(a, b):
    return pl.pallas_call(
        beside_kernel,
        out_shape=jax.ShapeDtypeStruct((a.shape[0], a.shape[1] + b.shape[1]), a.dtype),
        compiler_params=params(VMEM_MOST),
        name="beside",
        cost_estimate=cost(1),
    )(a, b)


def chip_exchange(blocks):
    groups = [[2 * i + c for i in range(DP // 2)] for c in range(2)]
    return lax.all_to_all(blocks, "dp", 0, 0, axis_index_groups=groups, tiled=True)


def body(
    inputs, spatial_q, spatial_k, spatial_v, out_weight, norm_gain, qkv_weight, grad_out, grad_resid
):
    block_shape = inputs.shape
    factor = (TOK * DP * SEQ) ** (-0.5)
    flat_in, q, k, v, dout, resid = (
        a.reshape(TOK, WIDTH)
        for a in (inputs, spatial_q, spatial_k, spatial_v, grad_out, grad_resid)
    )
    gain = norm_gain.reshape(1, WIDTH)
    me = lax.axis_index("seq")
    place_x, place_y = me // 2, me % 2
    order = jnp.stack(
        [((place_x + s) % XS) * 2 + y for y in (place_y, 1 - place_y) for s in (0, 3, 1, 2)]
        + [lax.axis_index("dp") % 2]
    ).astype(jnp.int32)

    weights = lax.all_gather(
        beside(out_weight, qkv_weight), "dp", axis=0, tiled=True
    )
    mixed = spatial_fwd(q, k, v)
    grad_heads = settle(
        lax.all_to_all(
            dout.reshape(TOK, SEQ, GROUP).transpose(1, 0, 2), "seq", 0, 0, tiled=True
        )
    )
    mixed_parts = gather_by_x(mixed)
    mixed_all = jnp.concatenate(mixed_parts, axis=0)
    weights, grad_heads, mixed_all = lax.optimization_barrier((weights, grad_heads, mixed_all))
    hidden, normed, wide_proj = out_norm(mixed, weights, flat_in, gain)
    normed_parts = gather_frames(normed)
    proj = [dot_nn(f, wide_proj).astype(BF) for f in whole_frames(normed_parts)]
    heads_out, dproj = temporal(order, proj, grad_heads)
    partner, pbehind, pahead, pfar = shares_of(dproj, wide_proj, 1)
    partner, pbehind, pahead, pfar, dproj = lax.optimization_barrier(
        (partner, pbehind, pahead, pfar, dproj)
    )
    qkv_share = qkv_product(normed_parts, dproj, factor)
    qkv_grad = lax.psum_scatter(qkv_share, "dp", scatter_dimension=0, tiled=True)
    pfar, pbehind, pahead = lax.optimization_barrier(
        (across_y(pfar), along_x(pbehind, -1), along_x(pahead, 1))
    )
    own, behind, ahead, far = shares_of(dproj, wide_proj, 0)
    sums = scatter_frames(own, behind, ahead, far + pfar, partner, pbehind, pahead)

    grad_input, groups = grad_input_call(sums, hidden, resid, gain, heads_out, factor)
    groups = lax.all_to_all(groups, "seq", 0, 0, tiled=True)
    grads = spatial_bwd(grad_input, weights, q, k, v)
    groups, *grads = lax.optimization_barrier((groups, *grads))
    mine, other = out_product(order, groups, mixed_all, factor)
    summed = mine + lax.ppermute(other, "dp", [(i, i ^ 1) for i in range(DP)])
    received = chip_exchange(summed)
    temporal_out = groups[:, :TOK, GROUPED:].transpose(1, 0, 2).reshape(TOK, WIDTH)
    gathered = lax.all_to_all(fold(received), "seq", 0, 0, tiled=True)
    gathered, qkv_grad = lax.optimization_barrier((gathered, qkv_grad.astype(F32)))
    out_grad, gain_grad = finish(gathered)
    return tuple(a.reshape(block_shape) for a in (hidden, temporal_out, grad_input, *grads)) + (
        qkv_grad,
        out_grad,
        gain_grad,
    )


def solution(mesh):
    tokens = P("dp", "seq", None, None, None)
    return jax.shard_map(
        body,
        mesh=mesh,
        in_specs=(
            tokens, tokens, tokens, tokens, P("dp", None), P(), P("dp", "seq"), tokens, tokens,
        ),
        out_specs=(
            tokens, tokens, tokens, tokens, tokens, tokens, P("dp", "seq"), P("dp", None), P(),
        ),
        check_vma=False,
    )
```

```python
import functools

import jax
import jax.numpy as jnp
from jax import lax
from jax.experimental import pallas as pl
from jax.experimental.pallas import tpu as pltpu
from jax.sharding import PartitionSpec as P

HEADS = 24
HDIM = 64
EPSILON = 1e-06
XS = 4
SEQ = 8
DP = 16
TOK = 128
WIDTH = HEADS * HDIM
GROUP = WIDTH // SEQ
LANE = 128
BF = jnp.bfloat16
F32 = jnp.float32
SCALE = HDIM**-0.5
VMEM_LIMIT = 20 * 1024 * 1024
VMEM_MOST = 58 * 1024 * 1024
HBM_RATE = 3_000_000


def params(limit=VMEM_LIMIT):
    return pltpu.CompilerParams(vmem_limit_bytes=limit)


def cost(micros):
    return pl.CostEstimate(flops=0, bytes_accessed=int(micros * HBM_RATE), transcendentals=0)


def dot_nt(a, b):
    return lax.dot_general(a, b, (((1,), (1,)), ((), ())), preferred_element_type=F32)


def dot_tn(a, b):
    return lax.dot_general(a, b, (((0,), (0,)), ((), ())), preferred_element_type=F32)


def dot_nn(a, b):
    return lax.dot_general(a, b, (((1,), (0,)), ((), ())), preferred_element_type=F32)


def spread(block, heads):
    lane = lax.broadcasted_iota(jnp.int32, block.shape, 1) // HDIM
    return jnp.concatenate(
        [jnp.where(lane == h, block, jnp.zeros_like(block)) for h in range(heads)], axis=0
    )


def pick(stacked, heads):
    rows = stacked.shape[0] // heads
    lane = lax.broadcasted_iota(jnp.int32, (rows, stacked.shape[1]), 1) // HDIM
    out = stacked[:rows]
    for h in range(1, heads):
        out = jnp.where(lane == h, stacked[h * rows : (h + 1) * rows], out)
    return out


def soft(scores, heads, valid=None):
    cols = scores.shape[1] // heads
    probs = []
    for h in range(heads):
        part = scores[:, h * cols : (h + 1) * cols] * SCALE
        if valid is not None:
            part = jnp.where(valid, part, -jnp.inf)
        raised = jnp.exp(part - jnp.max(part, axis=-1, keepdims=True))
        probs.append(raised / jnp.sum(raised, axis=-1, keepdims=True))
    return probs


def score_grad(probs, dprobs):
    cols = probs[0].shape[1]
    parts = []
    for h, prob in enumerate(probs):
        dpart = dprobs[:, h * cols : (h + 1) * cols]
        inner = jnp.sum(prob * dpart, axis=-1, keepdims=True)
        parts.append((prob * (dpart - inner) * SCALE).astype(BF))
    return jnp.concatenate(parts, axis=1)


def rounded(probs):
    return jnp.concatenate([p.astype(BF) for p in probs], axis=1)


PAIRS = 4


def spatial_fwd_kernel(q_ref, k_ref, v_ref, out_ref):
    for pair in range(PAIRS):
        cols = slice(pair * LANE, (pair + 1) * LANE)
        probs = soft(dot_nt(q_ref[:, cols], spread(k_ref[:, cols], 2)), 2)
        out_ref[:, cols] = dot_nn(rounded(probs), spread(v_ref[:, cols], 2)).astype(BF)


def spatial_fwd(q, k, v):
    spec = pl.BlockSpec((TOK, PAIRS * LANE), lambda i: (0, i))
    return pl.pallas_call(
        spatial_fwd_kernel,
        grid=(WIDTH // (PAIRS * LANE),),
        in_specs=[spec] * 3,
        out_specs=spec,
        out_shape=jax.ShapeDtypeStruct((TOK, WIDTH), BF),
        compiler_params=params(VMEM_MOST),
        name="spatial_fwd",
        cost_estimate=cost(4),
    )(q, k, v)


def spatial_bwd_kernel(gi_ref, w_ref, q_ref, k_ref, v_ref, dq_ref, dk_ref, dv_ref):
    dmixed = dot_nn(gi_ref[...], w_ref[...]).astype(BF)
    for pair in range(PAIRS):
        cols = slice(pair * LANE, (pair + 1) * LANE)
        q, dout = q_ref[:, cols], dmixed[:, cols]
        keys, values = spread(k_ref[:, cols], 2), spread(v_ref[:, cols], 2)
        probs = soft(dot_nt(q, keys), 2)
        dscores = score_grad(probs, dot_nt(dout, values))
        dv_ref[:, cols] = pick(dot_tn(rounded(probs), dout), 2).astype(BF)
        dq_ref[:, cols] = dot_nn(dscores, keys).astype(BF)
        dk_ref[:, cols] = pick(dot_tn(dscores, q), 2).astype(BF)


def spatial_bwd(grad_input, whole_out, q, k, v):
    spec = pl.BlockSpec((TOK, PAIRS * LANE), lambda i: (0, i))
    return pl.pallas_call(
        spatial_bwd_kernel,
        grid=(WIDTH // (PAIRS * LANE),),
        in_specs=[
            pl.BlockSpec((TOK, WIDTH), lambda i: (0, 0)),
            pl.BlockSpec((WIDTH, PAIRS * LANE), lambda i: (0, i)),
        ]
        + [spec] * 3,
        out_specs=[spec] * 3,
        out_shape=[jax.ShapeDtypeStruct((TOK, WIDTH), BF)] * 3,
        compiler_params=params(VMEM_MOST),
        name="spatial_bwd",
        cost_estimate=cost(9),
    )(grad_input, whole_out, q, k, v)


OUT_BLOCK = 512


PADDED = 256
THREE = 3 * PADDED


def widen(block, out_ref):
    for j in range(3):
        for h in range(3):
            out_ref[:, j * PADDED + h * HDIM : j * PADDED + (h + 1) * HDIM] = block[
                :, (h * 3 + j) * HDIM : (h * 3 + j + 1) * HDIM
            ]
        out_ref[:, j * PADDED + GROUP : (j + 1) * PADDED] = jnp.zeros(
            (block.shape[0], PADDED - GROUP), BF
        )


def out_norm_kernel(mixed_ref, w_ref, in_ref, gain_ref, hidden_ref, normed_ref, wide_ref):
    step = pl.program_id(0)
    block = in_ref[...].astype(F32) + dot_nt(mixed_ref[...], w_ref[:, :WIDTH])
    start = pl.multiple_of(step * OUT_BLOCK, OUT_BLOCK)
    hidden_ref[:, pl.ds(start, OUT_BLOCK)] = block.astype(BF)
    widen(w_ref[:, WIDTH:], wide_ref)

    @pl.when(step == pl.num_programs(0) - 1)
    def _():
        wide = hidden_ref[...].astype(F32)
        inverse = lax.rsqrt(jnp.mean(wide * wide, axis=-1, keepdims=True) + EPSILON)
        normed_ref[...] = (wide * inverse * gain_ref[...]).astype(BF)


def out_norm(mixed, weights, inputs, gain):
    whole = pl.BlockSpec((TOK, WIDTH), lambda i: (0, 0))
    return pl.pallas_call(
        out_norm_kernel,
        grid=(WIDTH // OUT_BLOCK,),
        in_specs=[
            whole,
            pl.BlockSpec((OUT_BLOCK, weights.shape[1]), lambda i: (i, 0)),
            pl.BlockSpec((TOK, OUT_BLOCK), lambda i: (0, i)),
            pl.BlockSpec((1, WIDTH), lambda i: (0, 0)),
        ],
        out_specs=[whole, whole, pl.BlockSpec((OUT_BLOCK, THREE), lambda i: (i, 0))],
        out_shape=[jax.ShapeDtypeStruct((TOK, WIDTH), BF)] * 2
        + [jax.ShapeDtypeStruct((WIDTH, THREE), BF)],
        compiler_params=params(VMEM_MOST),
        name="out_norm",
        cost_estimate=cost(5),
    )(mixed, weights, inputs, gain)


POS = 16
CHAINS = 8


def temporal_block(q, keys, values, dout, valid):
    keys, values = spread(keys, 3), spread(values, 3)
    probs = soft(dot_nt(q, keys), 3, valid)
    prob_round = rounded(probs)
    dscores = score_grad(probs, dot_nt(dout, values))
    return dot_nn(prob_round, values).astype(BF), (
        dot_nn(dscores, keys).astype(BF),
        pick(dot_tn(dscores, q), 3).astype(BF),
        pick(dot_tn(prob_round, dout), 3).astype(BF),
    )


def temporal_kernel(order_ref, *refs):
    proj, (grad_ref, out_ref, dproj_ref) = refs[:SEQ], refs[SEQ:]
    shape = (SEQ * POS, SEQ * POS)
    valid = (
        lax.broadcasted_iota(jnp.int32, shape, 0) % POS
        == lax.broadcasted_iota(jnp.int32, shape, 1) % POS
    )
    for chain in range(CHAINS):
        place = slice(chain * POS, (chain + 1) * POS)

        def rows(j):
            return jnp.concatenate(
                [p[place, j * PADDED : j * PADDED + GROUP] for p in proj], axis=0
            )

        dout = jnp.concatenate([grad_ref[order_ref[r], place] for r in range(SEQ)], axis=0)
        heads_out, grads = temporal_block(rows(0), rows(1), rows(2), dout, valid)
        for r in range(SEQ):
            here = slice(r * POS, (r + 1) * POS)
            out_ref[order_ref[r], place] = heads_out[here]
            for j in range(3):
                dproj_ref[r, place, j * PADDED : j * PADDED + GROUP] = grads[j][here]
                dproj_ref[r, place, j * PADDED + GROUP : (j + 1) * PADDED] = jnp.zeros(
                    (POS, PADDED - GROUP), BF
                )


def temporal(order, proj, grad_heads):
    rows = CHAINS * POS
    frame = pl.BlockSpec((rows, THREE), lambda i, o: (i, 0))
    heads = pl.BlockSpec((SEQ, rows, GROUP), lambda i, o: (0, i, 0))
    return pl.pallas_call(
        temporal_kernel,
        grid_spec=pltpu.PrefetchScalarGridSpec(
            num_scalar_prefetch=1,
            grid=(TOK // rows,),
            in_specs=[frame] * SEQ + [heads],
            out_specs=[heads, pl.BlockSpec((SEQ, rows, THREE), lambda i, o: (0, i, 0))],
        ),
        out_shape=[
            jax.ShapeDtypeStruct((SEQ, TOK, GROUP), BF),
            jax.ShapeDtypeStruct((SEQ, TOK, THREE), BF),
        ],
        compiler_params=params(),
        name="temporal",
        cost_estimate=cost(8),
    )(order, *proj, grad_heads)


SHARE_COLS = 512


def shares_kernel(dproj_ref, w_ref, *outs):
    left = dproj_ref[...].reshape(len(outs) * TOK, THREE)
    full = dot_nt(left, w_ref[...]).astype(BF)
    for r, out in enumerate(outs):
        out[...] = full[r * TOK : (r + 1) * TOK]


def shares_of(dproj, wide_proj, half):
    count = SEQ // 2
    return pl.pallas_call(
        shares_kernel,
        grid=(WIDTH // SHARE_COLS,),
        in_specs=[
            pl.BlockSpec((count, TOK, THREE), lambda i: (half, 0, 0)),
            pl.BlockSpec((SHARE_COLS, THREE), lambda i: (i, 0)),
        ],
        out_specs=[pl.BlockSpec((TOK, SHARE_COLS), lambda i: (0, i))] * count,
        out_shape=[jax.ShapeDtypeStruct((TOK, WIDTH), BF)] * count,
        compiler_params=params(),
        name="shares",
        cost_estimate=cost(2),
    )(dproj, wide_proj)


GRAD_ROWS = 384


def qkv_grad_kernel(factor, *refs):
    frames, dproj_ref, out_ref = refs[:-2], refs[-2], refs[-1]
    left = jnp.concatenate([f[...] for f in frames], axis=0)
    right = dproj_ref[...].reshape(SEQ * TOK, THREE)
    full = (dot_tn(left, right) * factor).astype(BF)
    for j in range(3):
        for h in range(3):
            out_ref[:, (h * 3 + j) * HDIM : (h * 3 + j + 1) * HDIM] = full[
                :, j * PADDED + h * HDIM : j * PADDED + (h + 1) * HDIM
            ]


def qkv_product(frames, dproj, factor):
    return pl.pallas_call(
        functools.partial(qkv_grad_kernel, factor),
        grid=(WIDTH // GRAD_ROWS,),
        in_specs=[pl.BlockSpec((f.shape[0], GRAD_ROWS), lambda i: (0, i)) for f in frames]
        + [pl.BlockSpec((SEQ, TOK, THREE), lambda i: (0, 0, 0))],
        out_specs=pl.BlockSpec((GRAD_ROWS, 3 * GROUP), lambda i: (i, 0)),
        out_shape=jax.ShapeDtypeStruct((WIDTH, 3 * GROUP), BF),
        compiler_params=params(12 * 1024 * 1024),
        name="qkv_product",
        cost_estimate=cost(5),
    )(*frames, dproj)


SHARE = 12
SLOT = 16
FOUR = 4
EXTRA = 16
GROUPED = DP * SHARE


def mover():
    size = FOUR * SHARE * SEQ
    source = lax.broadcasted_iota(jnp.int32, (size, size), 0)
    target = lax.broadcasted_iota(jnp.int32, (size, size), 1)
    group = target // (FOUR * SHARE)
    block = (target // SHARE) % FOUR
    wanted = block * (SHARE * SEQ) + group * SHARE + target % SHARE
    return jnp.where(source == wanted, 1.0, 0.0).astype(BF)


def two_parts(row):
    high = row.astype(BF)
    return high, (row - high.astype(F32)).astype(BF)


def grad_input_kernel(factor, sum_a, sum_b, sum_c, sum_d, hidden_ref, resid_ref, gain_ref,
                      heads_ref, out_ref, groups_ref):
    def wide(ref):
        return ref[...].astype(F32)

    dnormed = (wide(sum_a) + wide(sum_b) + wide(sum_c) + wide(sum_d)).astype(BF).astype(F32)
    hidden = wide(hidden_ref)
    inverse = lax.rsqrt(jnp.mean(hidden * hidden, axis=-1, keepdims=True) + EPSILON)
    unit = hidden * inverse
    gain_high, gain_low = two_parts(jnp.sum(dnormed * unit, axis=0, keepdims=True) * factor)
    scaled = dnormed * gain_ref[...]
    through = inverse * (scaled - unit * jnp.mean(scaled * unit, axis=-1, keepdims=True))
    grad = (wide(resid_ref) + through).astype(BF)
    out_ref[...] = grad
    row = lax.broadcasted_iota(jnp.int32, (EXTRA, WIDTH), 0)
    extra = jnp.where(row == 0, gain_high.astype(F32), jnp.where(row == 1, gain_low.astype(F32), 0.0))
    both = jnp.concatenate([grad, extra.astype(BF)], axis=0)
    move = mover()
    rows, cols = FOUR * SHARE * SEQ, FOUR * SHARE
    for four in range(DP // FOUR):
        moved = dot_nn(both[:, four * rows : (four + 1) * rows], move).astype(BF)
        for j in range(SEQ):
            groups_ref[j, :, four * cols : (four + 1) * cols] = moved[:, j * cols : (j + 1) * cols]
    groups_ref[:, :TOK, GROUPED:] = heads_ref[...]
    groups_ref[:, TOK:, GROUPED:] = jnp.zeros((SEQ, EXTRA, GROUP), BF)


def grad_input_call(sums, hidden, resid, gain, heads_out, factor):
    return pl.pallas_call(
        functools.partial(grad_input_kernel, factor),
        out_shape=[
            jax.ShapeDtypeStruct((TOK, WIDTH), BF),
            jax.ShapeDtypeStruct((SEQ, TOK + EXTRA, GROUPED + GROUP), BF),
        ],
        compiler_params=params(),
        name="grad_input",
        cost_estimate=cost(2),
    )(*sums, hidden, resid, gain, heads_out)


def out_product_kernel(factor, order_ref, groups_ref, mixed_ref, mine_ref, other_ref, turned):
    @pl.when(pl.program_id(0) == 0)
    def _():
        for r in range(SEQ):
            turned[:, r * TOK : (r + 1) * TOK] = groups_ref[order_ref[r], :TOK, :GROUPED].T

    product = dot_nn(turned[...], mixed_ref[...]) * factor
    cols = product.shape[1]
    extras = sum(groups_ref[r, TOK:, :GROUPED].astype(F32) for r in range(SEQ))
    gain_parts = jnp.concatenate(
        [part.astype(F32) for part in two_parts(extras[0:1] + extras[1:2])], axis=0
    )
    gain_parts = jnp.concatenate([gain_parts, jnp.zeros((2, cols - GROUPED), F32)], axis=1)
    gain_parts = jnp.where(pl.program_id(0) == 0, gain_parts, 0.0)
    tail = jnp.concatenate([gain_parts, jnp.zeros((SLOT - SHARE - 2, cols), F32)], axis=0)

    def block(d):
        return jnp.concatenate([product[d * SHARE : (d + 1) * SHARE], tail], axis=0).astype(BF)

    first_core = order_ref[SEQ] == 0
    for d in range(DP // 2):
        even, odd = block(2 * d), block(2 * d + 1)
        mine_ref[d] = jnp.where(first_core, even, odd)
        other_ref[d] = jnp.where(first_core, odd, even)


def out_product(order, groups, mixed_all, factor):
    cols = 512
    spec = pl.BlockSpec((DP // 2, SLOT, cols), lambda i, o: (0, 0, i))
    return pl.pallas_call(
        functools.partial(out_product_kernel, factor),
        grid_spec=pltpu.PrefetchScalarGridSpec(
            num_scalar_prefetch=1,
            grid=(WIDTH // cols,),
            in_specs=[
                pl.BlockSpec(groups.shape, lambda i, o: (0, 0, 0)),
                pl.BlockSpec((SEQ * TOK, cols), lambda i, o: (0, i)),
            ],
            out_specs=[spec, spec],
            scratch_shapes=[pltpu.VMEM((GROUPED, SEQ * TOK), BF)],
        ),
        out_shape=[jax.ShapeDtypeStruct((DP // 2, SLOT, WIDTH), BF)] * 2,
        compiler_params=params(),
        name="out_product",
        cost_estimate=cost(3),
    )(order, groups, mixed_all)


def fold_kernel(in_ref, out_ref):
    total = in_ref[0].astype(F32)
    for d in range(1, DP // 2):
        total = total + in_ref[d].astype(F32)
    high, low = two_parts(total[SHARE : SHARE + 1] + total[SHARE + 1 : SHARE + 2])
    turn = lax.broadcasted_iota(jnp.int32, total.shape, 0)
    total = jnp.where(turn == SHARE, high.astype(F32), total)
    total = jnp.where(turn == SHARE + 1, low.astype(F32), total).astype(BF)
    for j in range(SEQ):
        out_ref[j] = total


def fold(pieces):
    return pl.pallas_call(
        fold_kernel,
        out_shape=jax.ShapeDtypeStruct((SEQ, SLOT, WIDTH), BF),
        compiler_params=params(),
        name="fold",
        cost_estimate=cost(1.5),
    )(pieces)


def finish_kernel(in_ref, out_ref, gain_ref):
    out_ref[...] = jnp.concatenate(
        [in_ref[j].astype(F32)[:SHARE] for j in range(SEQ)], axis=0
    )
    move = mover()
    rows, cols = FOUR * SHARE * SEQ, FOUR * SHARE
    for four in range(DP // FOUR):
        left = jnp.concatenate(
            [in_ref[j, :, four * cols : (four + 1) * cols] for j in range(SEQ)], axis=1
        )
        back = dot_nt(left, move)
        gain_ref[pl.ds(four * rows, rows)] = back[SHARE] + back[SHARE + 1]


def finish(gathered):
    return pl.pallas_call(
        finish_kernel,
        out_shape=[
            jax.ShapeDtypeStruct((SEQ * SHARE, WIDTH), F32),
            jax.ShapeDtypeStruct((WIDTH,), F32),
        ],
        compiler_params=params(),
        name="finish",
        cost_estimate=cost(2),
    )(gathered)


def along_x(array, shift):
    pairs = [(i, ((i // 2 + shift) % XS) * 2 + i % 2) for i in range(SEQ)]
    return lax.ppermute(array, "seq", pairs)


def across_y(array):
    return lax.ppermute(array, "seq", [(i, i ^ 1) for i in range(SEQ)])


HALF = TOK // 2


def gather_frames(own):
    behind, ahead, partner = along_x(own, 1), along_x(own, -1), across_y(own)
    far_top, far_low = along_x(behind[:HALF], 1), along_x(ahead[HALF:], -1)
    partner_behind, partner_ahead = along_x(partner, 1), along_x(partner, -1)
    return (
        own, behind, ahead, far_top, far_low,
        partner, partner_behind, partner_ahead, across_y(far_top), across_y(far_low),
    )


def gather_by_x(own):
    partner, behind, ahead, far = across_y(own), along_x(own, 1), along_x(own, -1), along_x(own, 2)
    return (
        own, behind, ahead, far,
        partner, along_x(partner, 1), along_x(partner, -1), along_x(partner, 2),
    )


def whole_frames(parts):
    own, behind, ahead, top, low, partner, pbehind, pahead, ptop, plow = parts
    return (
        own, behind, ahead, jnp.concatenate([top, low], axis=0),
        partner, pbehind, pahead, jnp.concatenate([ptop, plow], axis=0),
    )


def scatter_frames(own, behind, ahead, far, partner, from_pbehind, from_pahead):
    partner = partner + from_pbehind + from_pahead
    top, low = along_x(far[:HALF], -1), along_x(far[HALF:], 1)
    behind = jnp.concatenate([behind[:HALF] + top, behind[HALF:]], axis=0)
    ahead = jnp.concatenate([ahead[:HALF], ahead[HALF:] + low], axis=0)
    return own, across_y(partner), along_x(behind, -1), along_x(ahead, 1)


def settle_kernel(in_ref, out_ref):
    out_ref[...] = in_ref[...]


def settle(array):
    return pl.pallas_call(
        settle_kernel,
        out_shape=jax.ShapeDtypeStruct(array.shape, array.dtype),
        compiler_params=params(),
        name="settle",
        cost_estimate=cost(1),
    )(array)


def beside_kernel(a_ref, b_ref, out_ref):
    out_ref[:, : a_ref.shape[1]] = a_ref[...]
    out_ref[:, a_ref.shape[1] :] = b_ref[...]


def beside(a, b):
    return pl.pallas_call(
        beside_kernel,
        out_shape=jax.ShapeDtypeStruct((a.shape[0], a.shape[1] + b.shape[1]), a.dtype),
        compiler_params=params(VMEM_MOST),
        name="beside",
        cost_estimate=cost(1),
    )(a, b)


def chip_exchange(blocks):
    groups = [[2 * i + c for i in range(DP // 2)] for c in range(2)]
    return lax.all_to_all(blocks, "dp", 0, 0, axis_index_groups=groups, tiled=True)


def body(
    inputs, spatial_q, spatial_k, spatial_v, out_weight, norm_gain, qkv_weight, grad_out, grad_resid
):
    block_shape = inputs.shape
    factor = (TOK * DP * SEQ) ** (-0.5)
    flat_in, q, k, v, dout, resid = (
        a.reshape(TOK, WIDTH)
        for a in (inputs, spatial_q, spatial_k, spatial_v, grad_out, grad_resid)
    )
    gain = norm_gain.reshape(1, WIDTH)
    me = lax.axis_index("seq")
    place_x, place_y = me // 2, me % 2
    order = jnp.stack(
        [((place_x + s) % XS) * 2 + y for y in (place_y, 1 - place_y) for s in (0, 3, 1, 2)]
        + [lax.axis_index("dp") % 2]
    ).astype(jnp.int32)

    weights = lax.all_gather(
        beside(out_weight, qkv_weight), "dp", axis=0, tiled=True
    )
    mixed = spatial_fwd(q, k, v)
    grad_heads = settle(
        lax.all_to_all(
            dout.reshape(TOK, SEQ, GROUP).transpose(1, 0, 2), "seq", 0, 0, tiled=True
        )
    )
    mixed_parts = gather_by_x(mixed)
    mixed_all = jnp.concatenate(mixed_parts, axis=0)
    weights, grad_heads, mixed_all = lax.optimization_barrier((weights, grad_heads, mixed_all))
    hidden, normed, wide_proj = out_norm(mixed, weights, flat_in, gain)
    normed_parts = gather_frames(normed)
    proj = [dot_nn(f, wide_proj).astype(BF) for f in whole_frames(normed_parts)]
    heads_out, dproj = temporal(order, proj, grad_heads)
    partner, pbehind, pahead, pfar = shares_of(dproj, wide_proj, 1)
    partner, pbehind, pahead, pfar, dproj = lax.optimization_barrier(
        (partner, pbehind, pahead, pfar, dproj)
    )
    qkv_share = qkv_product(normed_parts, dproj, factor)
    qkv_grad = lax.psum_scatter(qkv_share, "dp", scatter_dimension=0, tiled=True)
    pfar, pbehind, pahead = lax.optimization_barrier(
        (across_y(pfar), along_x(pbehind, -1), along_x(pahead, 1))
    )
    own, behind, ahead, far = shares_of(dproj, wide_proj, 0)
    sums = scatter_frames(own, behind, ahead, far + pfar, partner, pbehind, pahead)

    grad_input, groups = grad_input_call(sums, hidden, resid, gain, heads_out, factor)
    groups = lax.all_to_all(groups, "seq", 0, 0, tiled=True)
    grads = spatial_bwd(grad_input, weights, q, k, v)
    groups, *grads = lax.optimization_barrier((groups, *grads))
    mine, other = out_product(order, groups, mixed_all, factor)
    summed = mine + lax.ppermute(other, "dp", [(i, i ^ 1) for i in range(DP)])
    received = chip_exchange(summed)
    temporal_out = groups[:, :TOK, GROUPED:].transpose(1, 0, 2).reshape(TOK, WIDTH)
    gathered = lax.all_to_all(fold(received), "seq", 0, 0, tiled=True)
    gathered, qkv_grad = lax.optimization_barrier((gathered, qkv_grad.astype(F32)))
    out_grad, gain_grad = finish(gathered)
    return tuple(a.reshape(block_shape) for a in (hidden, temporal_out, grad_input, *grads)) + (
        qkv_grad,
        out_grad,
        gain_grad,
    )


def solution(mesh):
    tokens = P("dp", "seq", None, None, None)
    return jax.shard_map(
        body,
        mesh=mesh,
        in_specs=(
            tokens, tokens, tokens, tokens, P("dp", None), P(), P("dp", "seq"), tokens, tokens,
        ),
        out_specs=(
            tokens, tokens, tokens, tokens, tokens, tokens, P("dp", "seq"), P("dp", None), P(),
        ),
        check_vma=False,
    )
```
